32 devices in a mesh: dp: 4 (over z), row: 4 (over y, x), col: 2 (over core).
Axes of the slice: x: 2, y: 2, z: 4, core: 2. Of those that a mesh axis runs over, the one named last changes fastest.
Arguments:
- block_input: float32 [4096, 2, 1024], P(('dp', 'row', 'col')), may hold values from -6 to 6
- seq_lengths: int32 [4, 2, 8], P('dp'), may hold values from 1 to 1017, as said below
- routes: int32 [4096, 2, 8], P(('dp', 'row', 'col')), may hold values from 0 to 31, all different within a row; in each aligned block of 256 rows (0 to 255, 256 to 511, ..., all dimensions but the last counted through in order) at most 128 rows name the same one
- norm1_gain: float32 [1024], replicated, may hold values from 0.5 to 1.5
- w_qkv: bfloat16 [1024, 2048], P('col', 'row'), may hold values from -0.25 to 0.25
- w_heads: bfloat16 [1024, 1024], P(('row', 'col')), may hold values from -0.75 to 0.75
- norm2_gain: float32 [1024], replicated, may hold values from 0.5 to 1.5
- router: bfloat16 [1024, 32], replicated, may hold values from -0.09375 to 0.09375
- w_expert_in: bfloat16 [32, 1024, 1024], P('dp'), may hold values from -0.1875 to 0.1875
- w_expert_out: bfloat16 [32, 512, 1024], P('dp'), may hold values from -1 to 1
- out_grad: float32 [4096, 2, 1024], P(('dp', 'row', 'col')), may hold values from -6 to 6
Outputs:
- block_output: float32 [4096, 2, 1024], P(('dp', 'row', 'col'))
- input_grad: float32 [4096, 2, 1024], P(('dp', 'row', 'col'))
- norm1_grad: float32 [1024], replicated
- qkv_grad: float32 [1024, 2048], P('col', 'row')
- heads_grad: float32 [1024, 1024], P(('row', 'col'))
- norm2_grad: float32 [1024], replicated
- router_grad: float32 [1024, 32], replicated
- expert_in_grad: float32 [32, 1024, 1024], P('dp')
- expert_out_grad: float32 [32, 512, 1024], P('dp')
The draws below stay inside these ranges and needn't reach their ends.
Inputs may be any that keep to these rules, and one draw needn't show every extreme that they name: `seq_lengths`: the 8 lengths of each micro-batch of a token batch sum to 1024; in each of them one sequence begins within the first 128 places and ends within the last 128. `routes`: each row names 8 different experts. In the rows of one device (aligned blocks of 256 rows of the first two dimensions taken together) no expert is named more than 128 times.
All inputs are finite; a program needn't handle non-finite values.
Results may differ from the reference program's by a relative error of at most 0.023.
Values may be sent and summed in bfloat16 or wider, within the bound.
No kernel may reach another device: no remote copies, remote signals or barrier semaphores. Data moves between devices by JAX's collectives and lax.ppermute only.
A program may use at most 256 MiB of HBM per device.

```python
import math
import jax
import jax.numpy as jnp
import numpy as np
from jax import lax

D = 1024
QUERY_HEADS = 16
KEY_VALUE_HEADS = 8
HEAD_SIZE = 64
EXPERTS = 32
FF = 512
TOP = 8
MB = 2
TOK_MB = 128
SEQS = 8
PACK = 1024
TOKENS = 4096
QKV = 2048
MOST = 128
N_DP = 4
N_ROW = 4
N_COL = 2


def draw_seq_lengths(key, part):
    key = jax.random.fold_in(key, 7)
    key_long, key_extra, key_full = jax.random.split(key, 3)
    per_cap = (TOK_MB - 1) // (SEQS - 1)
    long_at = jax.random.randint(key_long, (N_DP, MB, 1), 0, SEQS)
    extra_len = jax.random.randint(key_extra, (N_DP, MB, SEQS), 0, per_cap)
    full_at = jax.random.randint(key_full, (), 0, N_DP * MB)
    pack_ids = jnp.arange(N_DP * MB, dtype=jnp.int32).reshape(N_DP, MB, 1)
    extra_len = jnp.where(pack_ids == full_at, 0, extra_len)
    slot_ids = jnp.arange(SEQS, dtype=jnp.int32).reshape(1, 1, SEQS)
    others = jnp.where(slot_ids == long_at, 0, 1 + extra_len)
    longest = PACK - jnp.sum(others, axis=2, keepdims=True)
    return jnp.where(slot_ids == long_at, longest, others).astype(jnp.int32)


def block_scale(key, extent, cuts, least, top_value):
    loudness = 1.0
    for dim, blocks in cuts:
        heights = jax.random.uniform(jax.random.fold_in(jax.random.fold_in(key, 6), dim), (blocks,), jnp.float32, least / len(cuts), top_value / len(cuts))
        loudness = loudness * jnp.repeat(jnp.exp(heights), extent[dim] // blocks).reshape((-1,) + (1,) * (len(extent) - 1 - dim))
    return loudness


def assign_block(rng, own, number, rows, number_of, top, most, lean):
    ranking = jax.random.permutation(rng, number_of)
    heavy_load, usual = shares(number_of, rows * top, most, lean, True), shares(number_of, rows * top, most, lean, False)
    places = jnp.arange(number_of)

    def named(tallies, turn):
        used = int((tallies > 0).sum())
        fixed = max(1, used // 4)
        moved = fixed + (places - fixed + turn * (used - fixed)) % max(1, number_of - fixed)
        return jnp.zeros((number_of,), jnp.int32).at[ranking[jnp.where(places < fixed, places, moved)]].set(jnp.asarray(tallies, jnp.int32))

    tallies = jnp.where(number % 4 == 0, named(heavy_load, number // 4), named(usual, number - number // 4 - 1))
    mixed = jax.random.permutation(jax.random.fold_in(own, 3), number_of)
    giver, sink = mixed[0:number_of // 2 * 2:2], mixed[1:number_of // 2 * 2:2]
    slack = jnp.minimum(tallies[giver] - 1, most - tallies[sink]) // 2
    slack = jnp.where((giver == ranking[0]) | (sink == ranking[0]) | (tallies[sink] == 0), 0, jnp.maximum(slack, 0))
    moved = jax.random.randint(jax.random.fold_in(own, 4), (number_of // 2,), 0, 1 << 20) % (slack + 1)
    tallies = tallies.at[giver].add(-moved).at[sink].add(moved)
    items = jnp.searchsorted(jnp.cumsum(tallies), jnp.arange(rows * top), side="right").astype(jnp.int32)
    table = items.reshape(top, rows).T
    table = table[jax.random.permutation(jax.random.fold_in(own, 1), rows)]
    turn = jax.random.randint(jax.random.fold_in(own, 2), (rows, 1), 0, top)
    return jnp.take_along_axis(table, (jnp.arange(top)[None, :] + turn) % top, axis=1)


def shares(amount, total, bound, lean, full):
    loads = [(1 << 20) // math.isqrt(rank ** lean) + 1 for rank in range(1, amount + 1)]
    largest = bound if full else min(bound, max(-(-total // amount), total * loads[0] // sum(loads)))
    least = 1 if total - largest >= amount - 1 else 0
    given, rest = [largest] + [least] * (amount - 1), total - largest - least * (amount - 1)
    while rest > 0:
        free = [i for i in range(1, amount) if given[i] < largest] or [i for i in range(1, amount) if given[i] < bound]
        mass, budget = sum([loads[i] for i in free]), rest
        for i in free:
            more = min(bound - given[i], max(1, budget * loads[i] // mass), rest)
            given[i] = given[i] + more
            rest = rest - more
    return np.array(given)


def bell_draw(rng, shape, deviation, reach, pieces=(), held_as=jnp.bfloat16):
    factor_of = block_scale(rng, shape, pieces, -0.22, 0.18) if pieces else 1.0
    values = jax.random.normal(rng, shape, jnp.float32) * deviation * factor_of
    return jnp.minimum(jnp.maximum(values, -reach), reach).astype(held_as)


def setup_inputs(seed: int = 0) -> dict:
    keys = jax.random.split(jax.random.key(seed), 12)
    block_input = bell_draw(keys[0], (TOKENS, MB, D), 1.0, 6.0, ((0, 32),), jnp.float32)
    seq_lengths = draw_seq_lengths(jax.random.fold_in(keys[11], 71), 0)
    routes_keys = jax.random.split(jax.random.fold_in(keys[2], 1), TOKENS * MB // (TOK_MB * MB))
    routes_turns = jax.random.permutation(jax.random.fold_in(keys[2], 3), TOKENS * MB // (TOK_MB * MB))
    routes = jax.vmap(lambda own, number: assign_block(jax.random.fold_in(keys[2], 2), own, number, TOK_MB * MB, EXPERTS, TOP, MOST, 1))(routes_keys, routes_turns).reshape((TOKENS, MB, TOP))
    norm1_gain = jnp.clip(1.0 + 0.1 * jax.random.normal(keys[3], (D,), jnp.float32), 0.5, 1.5)
    w_qkv = bell_draw(keys[4], (D, QKV), (D // 2) ** -0.5, 0.25, ((0, 2), (1, 4)))
    w_heads = bell_draw(keys[5], (QUERY_HEADS * HEAD_SIZE, D), (QUERY_HEADS * HEAD_SIZE // 16) ** -0.5, 0.75, ((0, 8),))
    norm2_gain = jnp.clip(1.0 + 0.1 * jax.random.normal(keys[6], (D,), jnp.float32), 0.5, 1.5)
    router = bell_draw(keys[7], (D, EXPERTS), (4 * D) ** -0.5, 0.09375)
    w_expert_in = bell_draw(keys[8], (EXPERTS, D, 2 * FF), D ** -0.5, 0.1875, ((0, 4),))
    w_expert_out = bell_draw(keys[9], (EXPERTS, FF, D), (FF // 16) ** -0.5, 1.0, ((0, 4),))
    out_grad = bell_draw(keys[10], (TOKENS, MB, D), 1.0, 6.0, ((0, 32),), jnp.float32)
    return dict(block_input=block_input, seq_lengths=seq_lengths, routes=routes, norm1_gain=norm1_gain, w_qkv=w_qkv, w_heads=w_heads, norm2_gain=norm2_gain, router=router, w_expert_in=w_expert_in, w_expert_out=w_expert_out, out_grad=out_grad)


highest = lax.Precision.HIGHEST
norm_eps = 1e-06
rope_base = 10000.0
neg_large = -1e+30

@jax.custom_vjp
def lower_bound(v):
    return lax.optimization_barrier(v.astype(jnp.bfloat16)).astype(jnp.float32)

@jax.custom_vjp
def low_back(v):
    return v

def low_keep(v):
    return (lower_bound(v), None)

def low_pass(kept, grad):
    return (grad,)

def back_keep(v):
    return (v, None)

def back_low(kept, grad):
    return (lower_bound(grad),)
lower_bound.defvjp(low_keep, low_pass)
low_back.defvjp(back_keep, back_low)

def rms_norm(value_rows, gain):
    factor = lax.rsqrt(lax.optimization_barrier(jnp.mean(value_rows * value_rows, axis=-1, keepdims=True)) + norm_eps)
    return value_rows * factor * gain

def apply_rotation(value_rows, cosine_table, sine_table):
    half_len = value_rows.shape[-1] // 2
    leading = value_rows[..., :half_len]
    second = value_rows[..., half_len:]
    return jnp.concatenate([leading * cosine_table - second * sine_table, second * cosine_table + leading * sine_table], axis=-1)

def pack_tables(lengths):
    seq_ends = jnp.cumsum(lengths).astype(jnp.int32)
    starts = (seq_ends - lengths).astype(jnp.int32)
    places = jnp.arange(PACK, dtype=jnp.int32)
    segment = lax.optimization_barrier(jnp.sum((places[:, None] >= seq_ends[None, :]).astype(jnp.int32), axis=1)).astype(jnp.int32)
    labels = jnp.arange(SEQS, dtype=jnp.int32)
    seq_start = lax.optimization_barrier(jnp.sum(jnp.where(segment[:, None] == labels[None, :], starts[None, :], 0), axis=1)).astype(jnp.int32)
    return (segment, places - seq_start)

def pack_attention(joined, segment, position):
    group_total = N_ROW * N_COL
    per_query = QUERY_HEADS // group_total
    queries_each_key = KEY_VALUE_HEADS // group_total
    group_width = joined.shape[1] // group_total
    parts = joined.reshape(PACK, group_total, group_width)
    queries = parts[:, :, :per_query * HEAD_SIZE].reshape(PACK, group_total, per_query, HEAD_SIZE)
    unrotated_key_rows = parts[:, :, per_query * HEAD_SIZE:(per_query + queries_each_key) * HEAD_SIZE].reshape(PACK, group_total, queries_each_key, HEAD_SIZE)
    plain_value_rows = parts[:, :, (per_query + queries_each_key) * HEAD_SIZE:].reshape(PACK, group_total, queries_each_key, HEAD_SIZE)
    inverse = jnp.exp(-(2.0 * jnp.arange(HEAD_SIZE // 2, dtype=jnp.float32) / HEAD_SIZE) * math.log(rope_base))
    angles = position.astype(jnp.float32)[:, None] * inverse[None, :]
    cosine_table = jnp.cos(angles)[:, None, None, :]
    sine_table = jnp.sin(angles)[:, None, None, :]
    queries = lower_bound(apply_rotation(queries, cosine_table, sine_table))
    rotated_key_rows = jnp.repeat(lower_bound(apply_rotation(unrotated_key_rows, cosine_table, sine_table)), QUERY_HEADS // KEY_VALUE_HEADS, axis=2)
    value_rows = jnp.repeat(lower_bound(plain_value_rows), QUERY_HEADS // KEY_VALUE_HEADS, axis=2)
    scores = jnp.einsum('tgqd,sgqd->gqts', queries, rotated_key_rows, precision=highest) * HEAD_SIZE ** (-0.5)
    places = jnp.arange(PACK, dtype=jnp.int32)
    visible = (segment[:, None] == segment[None, :]) & (places[:, None] >= places[None, :])
    scores = low_back(jnp.where(visible[None, None], scores, neg_large))
    row_max = lax.optimization_barrier(jnp.max(scores, axis=-1, keepdims=True))
    exp_part = jnp.exp(scores - row_max)
    weights = exp_part / lax.optimization_barrier(jnp.sum(exp_part, axis=-1, keepdims=True))
    mixed = jnp.einsum('gqts,sgqd->tgqd', lower_bound(weights), value_rows, precision=highest)
    return lower_bound(low_back(mixed)).reshape(PACK, QUERY_HEADS * HEAD_SIZE)

def pack_step(entry):
    return pack_attention(entry[0], entry[1], entry[2])

def expert_block(weights_in, weights_out, rows_in):
    activation = low_back(jnp.dot(rows_in, weights_in, precision=highest))
    gate_part = activation[:, :FF]
    up_part = activation[:, FF:]
    hidden = lower_bound(jax.nn.silu(gate_part) * up_part)
    return lower_bound(low_back(jnp.dot(hidden, weights_out, precision=highest)))

def reference(block_input, seq_lengths, routes, norm1_gain, w_qkv, w_heads, norm2_gain, router, w_expert_in, w_expert_out, out_grad):
    group_total = N_ROW * N_COL
    device_count = N_DP * group_total
    capacity = device_count * MOST
    rows_all = TOKENS * MB
    segment, position = jax.vmap(jax.vmap(pack_tables))(seq_lengths)
    segment = segment.reshape(N_DP * MB, PACK)
    position = position.reshape(N_DP * MB, PACK)
    chosen = routes.reshape(device_count, TOK_MB * MB * TOP).astype(jnp.int32)
    matches = (chosen[:, :, None] == jnp.arange(EXPERTS, dtype=jnp.int32)[None, None, :]).astype(jnp.int32)
    rank_of = lax.optimization_barrier(jnp.sum((jnp.cumsum(matches, axis=1).astype(jnp.int32) - 1) * matches, axis=2)).astype(jnp.int32)
    place_of = (jnp.arange(device_count, dtype=jnp.int32)[:, None] * MOST + rank_of).reshape(-1)
    pair_slot = (chosen.reshape(-1) * capacity + place_of).astype(jnp.int32)
    pair_row = (jnp.arange(rows_all * TOP, dtype=jnp.int32) // TOP).astype(jnp.int32)
    token_index = jnp.full((EXPERTS * capacity,), rows_all, jnp.int32).at[pair_slot].set(pair_row).reshape(EXPERTS, capacity)

    def forward(inputs, gain1, weights_qkv, weights_heads, gain2, weights_router, weights_in, weights_out):
        normed1 = lower_bound(rms_norm(inputs, gain1))
        joined = low_back(jnp.einsum('tmd,dc->tmc', normed1, weights_qkv, precision=highest))
        packs = joined.reshape(N_DP, PACK, MB, QKV).transpose(0, 2, 1, 3).reshape(N_DP * MB, PACK, QKV)
        head_out = lax.map(jax.checkpoint(pack_step), (packs, segment, position))
        head_out = head_out.reshape(N_DP, MB, PACK, QUERY_HEADS * HEAD_SIZE).transpose(0, 2, 1, 3).reshape(TOKENS, MB, QUERY_HEADS * HEAD_SIZE)
        mixed = inputs + low_back(jnp.einsum('tmc,cd->tmd', head_out, weights_heads, precision=highest))
        normed2 = lower_bound(rms_norm(mixed, gain2))
        logits = jnp.einsum('tmd,de->tme', normed2, weights_router, precision=highest)
        picked = jnp.take_along_axis(logits, routes, axis=2)
        row_max = lax.optimization_barrier(jnp.max(picked, axis=2, keepdims=True))
        exp_part = jnp.exp(picked - row_max)
        gate_weights = exp_part / lax.optimization_barrier(jnp.sum(exp_part, axis=2, keepdims=True))
        padded = jnp.concatenate([normed2.reshape(rows_all, D), jnp.zeros((1, D), jnp.float32)], axis=0)

        def one_expert(entry):
            rows_in = low_back(padded[entry[2]])
            return expert_block(entry[0], entry[1], rows_in)
        produced = lax.map(jax.checkpoint(one_expert), (weights_in, weights_out, token_index))
        pair_out = produced.reshape(EXPERTS * capacity, D)[pair_slot].reshape(TOKENS, MB, TOP, D)
        return mixed + lax.optimization_barrier(jnp.sum(gate_weights[..., None] * pair_out, axis=2))
    floats = (block_input.astype(jnp.float32), norm1_gain.astype(jnp.float32), w_qkv.astype(jnp.float32), w_heads.astype(jnp.float32), norm2_gain.astype(jnp.float32), router.astype(jnp.float32), w_expert_in.astype(jnp.float32), w_expert_out.astype(jnp.float32))
    block_output, pullback = jax.vjp(forward, floats[0], floats[1], floats[2], floats[3], floats[4], floats[5], floats[6], floats[7])
    grads = pullback(out_grad.astype(jnp.float32))
    return (block_output, grads[0], grads[1], grads[2], grads[3], grads[4], grads[5], grads[6], grads[7])
```

```python
import functools
import math

import jax
import jax.numpy as jnp
from jax import lax
from jax.experimental import pallas as pl
from jax.experimental.pallas import tpu as pltpu
from jax.sharding import PartitionSpec as P

HEAD_SIZE = 64
EXPERTS = 32
FF = 512
WIDTH = 1024
GROUP = 4
MOST = 128
TAIL = 16

norm_eps = 1e-06
rope_base = 10000.0
neg_large = -1e30
inv_root = HEAD_SIZE ** (-0.5)

f32 = jnp.float32
bf16 = jnp.bfloat16
PLANE = ("row", "col")


def dot(a, b):
    return lax.dot_general(a, b, (((1,), (0,)), ((), ())), preferred_element_type=f32)


def dot_nt(a, b):
    return lax.dot_general(a, b, (((1,), (1,)), ((), ())), preferred_element_type=f32)


def dot_tn(a, b):
    return lax.dot_general(a, b, (((0,), (0,)), ((), ())), preferred_element_type=f32)


def split_bits(value):
    high = value.astype(bf16)
    return high, (value - high.astype(f32)).astype(bf16)


def iota(shape, dim):
    return lax.broadcasted_iota(jnp.int32, shape, dim)


def params(mib, **more):
    return pltpu.CompilerParams(vmem_limit_bytes=mib * 1024 * 1024, **more)


def pack_tables(lengths, packed_length):
    seq_ends = jnp.cumsum(lengths, axis=1)
    starts = seq_ends - lengths
    places = jnp.arange(packed_length, dtype=jnp.int32)
    segment = jnp.sum((places[None, :, None] >= seq_ends[:, None, :]).astype(jnp.int32), axis=2)
    labels = jnp.arange(lengths.shape[1], dtype=jnp.int32)
    seq_start = jnp.sum(
        jnp.where(segment[:, :, None] == labels[None, None, :], starts[:, None, :], 0), axis=2
    )
    return (segment, places[None, :] - seq_start)


def swap_halves(value):
    lane = iota(value.shape, 1) % HEAD_SIZE
    width = value.shape[1]
    return jnp.where(
        lane < HEAD_SIZE // 2,
        pltpu.roll(value, width - HEAD_SIZE // 2, 1),
        pltpu.roll(value, HEAD_SIZE // 2, 1),
    )


def fold(value):
    return value + pltpu.roll(value, HEAD_SIZE, 1)


def twice(pair):
    rolled = pltpu.roll(pair, HEAD_SIZE, 1)
    first = iota(pair.shape, 1) < HEAD_SIZE
    return jnp.where(first, pair, rolled).astype(bf16), jnp.where(first, rolled, pair).astype(bf16)


def block_mask(seg_rows, seg_cols, offset, size, limit):
    same = seg_rows[offset : offset + size] == seg_cols[:, :limit]
    rows = iota((size, limit), 0) + offset
    return same & (rows >= iota((size, limit), 1))


Q_BLOCK = 256


def attn_fwd_kernel(x_ref, w_ref, cos_ref, sin_ref, segr_ref, segc_ref, qkv_ref, out_ref, lse_ref):
    devices, _, rows, width = x_ref.shape
    packed = devices * rows
    joined = dot(x_ref[:, 0].reshape(packed, width), w_ref[...])
    cosine, sine = cos_ref[0], sin_ref[0]
    first = iota((packed, 128), 1) < HEAD_SIZE
    query = joined[:, :128]
    pair = joined[:, 128:]
    query = query * cosine + swap_halves(query) * sine
    pair = jnp.where(first, pair * cosine + swap_halves(pair) * sine, pair)
    query = query.astype(bf16)
    pair16 = pair.astype(bf16)
    qkv_ref[0, :, :128] = query
    qkv_ref[0, :, 128:] = pair16
    keys, values = twice(pair16.astype(f32))
    seg_rows, seg_cols = segr_ref[0], segc_ref[0]
    lane = iota((Q_BLOCK, 128), 1)
    for offset in range(0, packed, Q_BLOCK):
        limit = offset + Q_BLOCK
        mask = block_mask(seg_rows, seg_cols, offset, Q_BLOCK, limit)
        outs, sums = [], []
        for head in range(2):
            mine = (lane < HEAD_SIZE) if head == 0 else (lane >= HEAD_SIZE)
            rows_q = jnp.where(mine, query[offset:limit], jnp.zeros((), bf16))
            scores = dot_nt(rows_q, keys[:limit]) * inv_root
            scores = jnp.where(mask, scores, neg_large)
            top = jnp.max(scores, axis=1, keepdims=True)
            part = jnp.exp(scores - top)
            total = jnp.sum(part, axis=1, keepdims=True)
            weights = (part * (1.0 / total)).astype(bf16)
            outs.append(dot(weights, values[:limit]))
            sums.append(top + jnp.log(total))
        merged = jnp.where(lane < HEAD_SIZE, outs[0], outs[1]).astype(bf16)
        out_ref[offset // rows : limit // rows, 0] = merged.reshape(Q_BLOCK // rows, rows, 128)
        lse_ref[0, offset:limit] = jnp.where(lane < HEAD_SIZE, sums[0], sums[1])


def attn_bwd_kernel(
    x_ref, w_ref, gain_ref, cos_ref, sin_ref, segr_ref, segc_ref, qkv_ref, lse_ref, grad_ref,
    joined_ref, weight_ref, total_ref, dk_ref, dv_ref,
):
    devices, _, rows, width = x_ref.shape
    packed = devices * rows
    m = pl.program_id(0)
    query = qkv_ref[0, :, :128]
    keys, values = twice(qkv_ref[0, :, 128:].astype(f32))
    seg_rows, seg_cols = segr_ref[0], segc_ref[0]
    grad = grad_ref[:, 0].reshape(packed, 128)
    lane = iota((Q_BLOCK, 128), 1)
    zero = jnp.zeros((), bf16)
    dk_ref[...] = jnp.zeros_like(dk_ref)
    dv_ref[...] = jnp.zeros_like(dv_ref)
    grad_query = []
    for offset in range(0, packed, Q_BLOCK):
        limit = offset + Q_BLOCK
        mask = block_mask(seg_rows, seg_cols, offset, Q_BLOCK, limit)
        parts = []
        for head in range(2):
            mine = (lane < HEAD_SIZE) if head == 0 else (lane >= HEAD_SIZE)
            rows_q = jnp.where(mine, query[offset:limit], zero)
            rows_g = jnp.where(mine, grad[offset:limit], zero)
            scores = dot_nt(rows_q, keys[:limit]) * inv_root
            at = head * HEAD_SIZE
            probs = jnp.exp(jnp.where(mask, scores, neg_large) - lse_ref[0, offset:limit, at : at + 1])
            grad_probs = dot_nt(rows_g, values[:limit])
            weighed = probs * grad_probs
            delta = jnp.sum(weighed, axis=1, keepdims=True)
            grad_scores = (weighed - probs * delta).astype(bf16)
            parts.append(dot(grad_scores, keys[:limit]))
            dk_ref[:limit] += dot_tn(grad_scores, rows_q)
            dv_ref[:limit] += dot_tn(probs.astype(bf16), rows_g)
        grad_query.append(jnp.where(lane < HEAD_SIZE, parts[0], parts[1]))
    dq = jnp.concatenate(grad_query, axis=0) * inv_root
    dk = fold(dk_ref[...]) * inv_root
    dv = fold(dv_ref[...])
    cosine, sine = cos_ref[0], sin_ref[0]
    first = iota((packed, 128), 1) < HEAD_SIZE
    dq = dq * cosine - swap_halves(dq) * sine
    dk = dk * cosine - swap_halves(dk) * sine
    joined = jnp.concatenate([dq, jnp.where(first, dk, dv)], axis=1).astype(bf16)
    joined_ref[:, 0] = joined.reshape(devices, rows, 256)
    part = dot_tn(x_ref[:, 0].reshape(packed, width), joined)

    @pl.when(m == 0)
    def _():
        total_ref[...] = part

    @pl.when(m > 0)
    def _():
        total_ref[...] += part

    @pl.when(m == pl.num_programs(0) - 1)
    def _():
        weight_ref[...] = total_ref[...].astype(bf16)


def wide_of_dense(dense):
    return jnp.concatenate([dense[8 * b : 8 * b + 8] for b in range(EXPERTS // 8)], axis=1)


def dense_of_wide(wide):
    part = wide.shape[1] // (EXPERTS // 8)
    return jnp.concatenate(
        [wide[:, b * part : (b + 1) * part] for b in range(EXPERTS // 8)], axis=0
    )


def token_fwd_kernel(heads_ref, w_ref, x_ref, gain_ref, router_ref, rank_ref, mixed_ref, send_ref, gates_ref):
    heads = jnp.concatenate([heads_ref[j] for j in range(heads_ref.shape[0])], axis=1)
    mixed = x_ref[...] + dot(heads, w_ref[...])
    mixed_ref[...] = mixed
    scale = lax.rsqrt(jnp.mean(mixed * mixed, axis=1, keepdims=True) + norm_eps)
    normed = (mixed * scale * gain_ref[...]).astype(bf16)
    rows = normed.shape[0]
    send_ref[:rows] = normed
    logits = dot_nt(router_ref[...], normed)
    used = rank_ref[...].astype(f32) >= 0
    logits = jnp.where(used, logits, neg_large)
    part = jnp.where(used, jnp.exp(logits - jnp.max(logits, axis=0, keepdims=True)), 0.0)
    gates = part / jnp.sum(part, axis=0, keepdims=True)
    gates_ref[...] = gates
    high, low = split_bits(wide_of_dense(gates))
    send_ref[rows:] = jnp.concatenate([high.astype(f32), low.astype(f32)], axis=0).astype(bf16)


def token_bwd_kernel(
    back_ref, mixed_ref, out_grad_ref, gates_ref, heads_ref, w_ref, gain_ref, router_ref, normed_ref,
    grad_mixed_ref, grad_heads_ref, sums_ref,
):
    rows = mixed_ref.shape[0]
    tail = back_ref[rows:].astype(f32)
    grad_gates = dense_of_wide(tail[:8] + tail[8:])
    gates = gates_ref[...]
    weighed = gates * grad_gates
    spread = weighed - gates * jnp.sum(weighed, axis=0, keepdims=True)
    high, low = split_bits(spread)
    router = router_ref[...]
    grad_normed = back_ref[:rows].astype(f32) + dot_tn(high, router) + dot_tn(low, router)
    normed = normed_ref[:rows]
    router_grad = dot(high, normed) + dot(low, normed)
    mixed = mixed_ref[...]
    scale = lax.rsqrt(jnp.mean(mixed * mixed, axis=1, keepdims=True) + norm_eps)
    lifted = grad_normed * gain_ref[...]
    gain_grad = jnp.sum(grad_normed * mixed * scale, axis=0, keepdims=True)
    inner = jnp.mean(lifted * mixed, axis=1, keepdims=True)
    grad_mixed = out_grad_ref[...] + scale * lifted - mixed * (scale * scale * scale * inner)
    grad_mixed_ref[...] = grad_mixed
    branch = grad_mixed.astype(bf16)
    grad_heads = dot_nt(branch, w_ref[...]).astype(bf16)
    count = heads_ref.shape[0]
    for j in range(count):
        grad_heads_ref[j] = grad_heads[:, j * 128 : (j + 1) * 128]
        sums_ref[j, :128] = dot_tn(heads_ref[j], branch).astype(bf16)
        part = router_grad[j * (EXPERTS // count) : (j + 1) * (EXPERTS // count)]
        rest = jnp.zeros((TAIL - part.shape[0] - 1, part.shape[1]), f32)
        sums_ref[j, 128:] = jnp.concatenate(
            [part, gain_grad if j == 0 else jnp.zeros_like(gain_grad), rest], axis=0
        ).astype(bf16)


def token_end_kernel(joined_ref, w_ref, x_ref, gain_ref, grad_mixed_ref, out_ref):
    total = dot_nt(joined_ref[0], w_ref[0])
    for j in range(1, joined_ref.shape[0]):
        total = total + dot_nt(joined_ref[j], w_ref[j])
    x = x_ref[...]
    scale = lax.rsqrt(jnp.mean(x * x, axis=1, keepdims=True) + norm_eps)
    lifted = total * gain_ref[...]
    inner = jnp.mean(lifted * x, axis=1, keepdims=True)
    out_ref[...] = grad_mixed_ref[...] + scale * lifted - x * (scale * scale * scale * inner)


def expert_kernel(
    here, my_ref, rank_ref, rows_ref, grads_ref, w_in_ref, w_out_ref,
    out_ref, back_ref, gin_ref, gout_ref,
    x_scr, g_scr, gate_scr, out_acc, back_acc, gg_acc, gin_acc, gout_acc,
):
    group, expert = pl.program_id(0), pl.program_id(1)
    chosen = my_ref[0] * here + expert
    tokens = grads_ref.shape[1]
    width = grads_ref.shape[2]
    last_expert = expert == here - 1

    @pl.when(expert == 0)
    def _():
        out_acc[...] = jnp.zeros_like(out_acc)
        back_acc[...] = jnp.zeros_like(back_acc)

    blocks = EXPERTS // 8
    spots = []
    for s in range(GROUP):
        rank = rank_ref[s].astype(f32)
        rank_row = jnp.sum(
            jnp.where(iota(rank.shape, 0) == chosen, rank, 0.0), axis=0, keepdims=True
        )
        wide = rows_ref[s, tokens:].astype(f32)
        wide = wide[:8] + wide[8:]
        gate_row = jnp.zeros((1, tokens), f32)
        for b in range(blocks):
            part = wide[:, b * tokens : (b + 1) * tokens]
            gate_row += jnp.sum(
                jnp.where(iota(part.shape, 0) + 8 * b == chosen, part, 0.0), axis=0, keepdims=True
            )
        hit = iota((MOST, tokens), 0) == rank_row.astype(jnp.int32)
        spot = jnp.where(hit, 1.0, 0.0).astype(bf16)
        spots.append((hit, spot))
        at = slice(s * MOST, (s + 1) * MOST)
        x_scr[at] = dot(spot, rows_ref[s, :tokens]).astype(bf16)
        g_scr[at] = dot(spot, grads_ref[s]).astype(bf16)
        gate_scr[at] = jnp.sum(jnp.where(hit, gate_row, 0.0), axis=1, keepdims=True)

    x, g, gate = x_scr[...], g_scr[...], gate_scr[...]
    act = dot(x, w_in_ref[0])
    gate_part, up_part = act[:, :FF], act[:, FF:]
    sig = jax.nn.sigmoid(gate_part)
    silu = gate_part * sig
    hidden = silu * up_part
    raw = dot_nt(g, w_out_ref[0])
    grad_gates = jnp.sum(hidden * raw, axis=1, keepdims=True)
    scaled = (hidden * gate).astype(bf16)
    produced = dot(scaled, w_out_ref[0]).astype(bf16)
    grad_hidden = raw * gate
    grad_act = jnp.concatenate(
        [grad_hidden * up_part * sig * (1.0 + gate_part * (1.0 - sig)), grad_hidden * silu], axis=1
    ).astype(bf16)
    grad_rows = dot_nt(grad_act, w_in_ref[0]).astype(bf16)
    gin = dot_tn(x, grad_act)
    gout = dot_tn(scaled, g)
    if gin_acc is None:
        gin_ref[0] = gin.astype(bf16)
        gout_ref[0] = gout.astype(bf16)
    else:

        @pl.when(group == 0)
        def _():
            gin_acc[...] = gin
            gout_acc[...] = gout

        @pl.when(group > 0)
        def _():
            gin_acc[...] += gin
            gout_acc[...] += gout

        @pl.when(group == pl.num_programs(0) - 1)
        def _():
            gin_ref[0] = gin_acc[...].astype(bf16)
            gout_ref[0] = gout_acc[...].astype(bf16)

    for s in range(GROUP):
        hit, spot = spots[s]
        at = slice(s * MOST, (s + 1) * MOST)
        out_acc[s] += dot_tn(spot, produced[at])
        back_acc[s] += dot_tn(spot, grad_rows[at])
        gg_acc[s, pl.ds(expert, 1)] = jnp.sum(
            jnp.where(hit, grad_gates[at], 0.0), axis=0, keepdims=True
        )

    @pl.when(last_expert)
    def _():
        for s in range(GROUP):
            out_ref[s] = out_acc[s].astype(bf16)
            back_ref[s, :tokens] = back_acc[s].astype(bf16)
            mine = gg_acc[s, :here]
            if here == 1:
                mine = jnp.broadcast_to(mine, (8, tokens))
            wide = jnp.concatenate([mine] * blocks, axis=1)
            index = iota(wide.shape, 1) // tokens * 8 + iota(wide.shape, 0)
            wide = jnp.where(index // here == my_ref[0], wide, 0.0)
            high, low = split_bits(wide)
            back_ref[s, tokens:] = jnp.concatenate(
                [high.astype(f32), low.astype(f32)], axis=0
            ).astype(bf16)


def run_experts(my, ranks, rows, grads, w_in, w_out):
    sources, tokens, width = grads.shape
    here = w_in.shape[0]
    groups = sources // GROUP
    assert here in (1, 8) and (groups == 1 or here == 1)
    full = rows.shape[1]
    summed = groups > 1
    scratch = [
        pltpu.VMEM((GROUP * MOST, width), bf16),
        pltpu.VMEM((GROUP * MOST, width), bf16),
        pltpu.VMEM((GROUP * MOST, 1), f32),
        pltpu.VMEM((GROUP, tokens, width), f32),
        pltpu.VMEM((GROUP, tokens, width), f32),
        pltpu.VMEM((GROUP, 8, tokens), f32),
    ]
    if summed:
        scratch += [pltpu.VMEM((width, 2 * FF), f32), pltpu.VMEM((FF, width), f32)]
    body = functools.partial(expert_kernel, here)
    if not summed:
        inner = body
        body = lambda *refs: inner(*refs, None, None)
    by_group = lambda g, e, my: (g, 0, 0)
    by_expert = lambda g, e, my: (e, 0, 0)
    one = lambda shape, index: pl.BlockSpec(shape, index, pipeline_mode=pl.Buffered(1))
    once = one if groups == 1 else pl.BlockSpec
    return pl.pallas_call(
        body,
        grid_spec=pltpu.PrefetchScalarGridSpec(
            num_scalar_prefetch=1,
            grid=(groups, here),
            in_specs=[
                once((GROUP, EXPERTS, tokens), by_group),
                once((GROUP, full, width), by_group),
                once((GROUP, tokens, width), by_group),
                pl.BlockSpec((1, width, 2 * FF), by_expert),
                pl.BlockSpec((1, FF, width), by_expert),
            ],
            out_specs=[
                once((GROUP, tokens, width), by_group),
                once((GROUP, full, width), by_group),
                pl.BlockSpec((1, width, 2 * FF), by_expert),
                pl.BlockSpec((1, FF, width), by_expert),
            ],
            scratch_shapes=scratch,
        ),
        out_shape=[
            jax.ShapeDtypeStruct((sources, tokens, width), bf16),
            jax.ShapeDtypeStruct((sources, full, width), bf16),
            jax.ShapeDtypeStruct((here, width, 2 * FF), bf16),
            jax.ShapeDtypeStruct((here, FF, width), bf16),
        ],
        compiler_params=params(56),
        cost_estimate=pl.CostEstimate(
            flops=here * groups * 512 * 9_400_000, bytes_accessed=60_000_000, transcendentals=0
        ),
        name="experts",
    )(my, ranks, rows, grads, w_in, w_out)


def body(
    block_input,
    seq_lengths,
    routes,
    norm1_gain,
    w_qkv,
    w_heads,
    norm2_gain,
    router,
    w_expert_in,
    w_expert_out,
    out_grad,
):
    tok_rows, batches, width = block_input.shape
    dp_size = lax.axis_size("dp")
    plane = lax.axis_size("row") * lax.axis_size("col")
    packed = tok_rows * plane
    tokens = tok_rows * batches
    dp_at = lax.axis_index("dp").astype(jnp.int32)
    sds = jax.ShapeDtypeStruct

    x = jnp.transpose(block_input, (1, 0, 2)).reshape(tokens, width)
    og = jnp.transpose(out_grad, (1, 0, 2)).reshape(tokens, width)
    scale1 = lax.rsqrt(jnp.mean(x * x, axis=1, keepdims=True) + norm_eps)
    normed1 = (x * scale1 * norm1_gain).astype(bf16)
    gathered = lax.all_gather(normed1, PLANE, axis=0, tiled=False).reshape(
        plane, batches, tok_rows, width
    )
    w_group = lax.all_to_all(w_qkv, "col", split_axis=1, concat_axis=0, tiled=True)
    w_heads_all = lax.all_gather(w_heads, PLANE, axis=0, tiled=True)
    w_qkv_all = lax.all_gather(w_group, PLANE, axis=0, tiled=False)
    grads_in = lax.all_gather(og.astype(bf16), "dp", axis=0, tiled=False)

    flat_routes = jnp.transpose(routes, (1, 0, 2)).reshape(tokens, -1)
    used = jnp.any(
        flat_routes[None] == jnp.arange(EXPERTS, dtype=jnp.int32)[:, None, None], axis=2
    )
    before = (
        jnp.arange(tokens, dtype=jnp.int32)[:, None] < jnp.arange(tokens, dtype=jnp.int32)[None, :]
    )
    counted = jnp.dot(used.astype(bf16), before.astype(bf16), preferred_element_type=f32)
    rank = jnp.where(used, counted, -1.0).astype(bf16)
    ranks = lax.all_gather(rank, "dp", axis=0, tiled=False)

    segment, position = pack_tables(seq_lengths[0], packed)
    inverse = jnp.exp(
        -(2.0 * jnp.arange(HEAD_SIZE // 2, dtype=f32) / HEAD_SIZE) * math.log(rope_base)
    )
    angles = position.astype(f32)[:, :, None] * inverse[None, None, :]
    cosine, sine = jnp.cos(angles), jnp.sin(angles)
    cosine = jnp.concatenate([cosine] * 4, axis=2)
    sine = jnp.concatenate([-sine, sine, -sine, sine], axis=2)
    seg_rows, seg_cols = segment[:, :, None], segment[:, None, :]

    per_m = lambda m: (m, 0, 0)
    const = lambda m: (0, 0)
    x_spec = pl.BlockSpec((plane, 1, tok_rows, width), lambda m: (0, m, 0, 0))
    table_specs = [
        pl.BlockSpec((1, packed, 128), per_m),
        pl.BlockSpec((1, packed, 128), per_m),
        pl.BlockSpec((1, packed, 1), per_m),
        pl.BlockSpec((1, 1, packed), per_m),
    ]
    qkv, head_out, lse = pl.pallas_call(
        attn_fwd_kernel,
        grid=(batches,),
        in_specs=[x_spec, pl.BlockSpec((width, 256), const), *table_specs],
        out_specs=[
            pl.BlockSpec((1, packed, 256), per_m),
            pl.BlockSpec((plane, 1, tok_rows, 128), lambda m: (0, m, 0, 0)),
            pl.BlockSpec((1, packed, 128), per_m),
        ],
        out_shape=[
            sds((batches, packed, 256), bf16),
            sds((plane, batches, tok_rows, 128), bf16),
            sds((batches, packed, 128), f32),
        ],
        compiler_params=params(48),
        name="attn_fwd",
    )(gathered, w_group, cosine, sine, seg_rows, seg_cols)

    heads = lax.all_to_all(
        head_out.reshape(plane, tokens, 128), PLANE, split_axis=0, concat_axis=0, tiled=True
    )
    gain1, gain2 = norm1_gain.reshape(1, width), norm2_gain.reshape(1, width)
    router_t = jnp.transpose(router)
    mixed, send, gates = pl.pallas_call(
        token_fwd_kernel,
        out_shape=[
            sds((tokens, width), f32),
            sds((tokens + TAIL, width), bf16),
            sds((EXPERTS, tokens), f32),
        ],
        compiler_params=params(32),
        name="token_fwd",
    )(heads, w_heads_all, x, gain2, router_t, rank)

    rows_in = lax.all_gather(send, "dp", axis=0, tiled=False)
    produced, back, grad_w_in, grad_w_out = run_experts(
        dp_at.reshape(1), ranks, rows_in, grads_in, w_expert_in, w_expert_out
    )
    back = lax.psum_scatter(
        back.reshape(dp_size * (tokens + TAIL), width), "dp", scatter_dimension=0, tiled=True
    )
    produced = lax.psum_scatter(
        produced.reshape(dp_size * tokens, width), "dp", scatter_dimension=0, tiled=True
    )
    block_output = mixed + produced.astype(f32)

    grad_mixed, grad_heads, sums = pl.pallas_call(
        token_bwd_kernel,
        out_shape=[
            sds((tokens, width), f32),
            sds((plane, tokens, 128), bf16),
            sds((plane, 128 + TAIL, width), bf16),
        ],
        compiler_params=params(40),
        name="token_bwd",
    )(back, mixed, og, gates, heads, w_heads_all, gain2, router_t, send)

    grad_heads = lax.all_to_all(grad_heads, PLANE, split_axis=0, concat_axis=0, tiled=True)
    grad_joined, grad_w_qkv = pl.pallas_call(
        attn_bwd_kernel,
        grid=(batches,),
        in_specs=[
            x_spec,
            pl.BlockSpec((width, 256), const),
            pl.BlockSpec((1, width), const),
            *table_specs,
            pl.BlockSpec((1, packed, 256), per_m),
            pl.BlockSpec((1, packed, 128), per_m),
            pl.BlockSpec((plane, 1, tok_rows, 128), lambda m: (0, m, 0, 0)),
        ],
        out_specs=[
            pl.BlockSpec((plane, 1, tok_rows, 256), lambda m: (0, m, 0, 0)),
            pl.BlockSpec((width, 256), const),
        ],
        out_shape=[sds((plane, batches, tok_rows, 256), bf16), sds((width, 256), bf16)],
        scratch_shapes=[
            pltpu.VMEM((width, 256), f32),
            pltpu.VMEM((packed, 128), f32),
            pltpu.VMEM((packed, 128), f32),
        ],
        compiler_params=params(48),
        name="attn_bwd",
    )(
        gathered, w_group, gain1, cosine, sine, seg_rows, seg_cols, qkv, lse,
        grad_heads.reshape(plane, batches, tok_rows, 128),
    )

    grad_joined = lax.all_to_all(
        grad_joined.reshape(plane, tokens, 256), PLANE, split_axis=0, concat_axis=0, tiled=True
    )
    input_grad = pl.pallas_call(
        token_end_kernel,
        out_shape=sds((tokens, width), f32),
        compiler_params=params(32),
        name="token_end",
    )(grad_joined, w_qkv_all, x, gain1, grad_mixed)

    grad_w_in = lax.psum(grad_w_in, PLANE).astype(f32)
    grad_w_out = lax.psum(grad_w_out, PLANE).astype(f32)
    sums = lax.psum_scatter(
        sums.reshape(plane * (128 + TAIL), width), PLANE, scatter_dimension=0, tiled=True
    )
    sums = lax.psum(sums, "dp")
    heads_grad = sums[:128].astype(f32)
    rest = lax.all_gather(sums[128:], PLANE, axis=0, tiled=False).astype(f32)
    per = EXPERTS // plane
    router_grad = jnp.transpose(rest[:, :per].reshape(EXPERTS, width))
    norm2_grad = rest[0, per]
    grad_w_qkv = lax.all_to_all(grad_w_qkv, "col", split_axis=0, concat_axis=1, tiled=True)
    grad_w_qkv = lax.psum(grad_w_qkv, "dp").astype(f32)
    part = jnp.sum(grad_w_qkv * w_qkv.astype(f32), axis=1)
    half = part.shape[0]
    at = lax.axis_index("col") * half
    norm1_grad = lax.psum(
        lax.dynamic_update_slice(jnp.zeros((width,), f32), part, (at,)), PLANE
    ) / norm1_gain

    def placed(value):
        return jnp.transpose(value.reshape(batches, tok_rows, width), (1, 0, 2))

    return (
        placed(block_output),
        placed(input_grad),
        norm1_grad,
        grad_w_qkv,
        heads_grad,
        norm2_grad,
        router_grad,
        grad_w_in,
        grad_w_out,
    )


def solution(mesh):
    return jax.shard_map(
        body,
        mesh=mesh,
        in_specs=(
            P(("dp", "row", "col"), None, None),
            P("dp", None, None),
            P(("dp", "row", "col"), None, None),
            P(),
            P("col", "row"),
            P(("row", "col"), None),
            P(),
            P(),
            P("dp", None, None),
            P("dp", None, None),
            P(("dp", "row", "col"), None, None),
        ),
        out_specs=(
            P(("dp", "row", "col"), None, None),
            P(("dp", "row", "col"), None, None),
            P(),
            P("col", "row"),
            P(("row", "col"), None),
            P(),
            P(),
            P("dp", None, None),
            P("dp", None, None),
        ),
        check_vma=False,
    )
```

```python
import functools
import math

import jax
import jax.numpy as jnp
from jax import lax
from jax.experimental import pallas as pl
from jax.experimental.pallas import tpu as pltpu
from jax.sharding import PartitionSpec as P

HEAD_SIZE = 64
EXPERTS = 32
FF = 512
WIDTH = 1024
GROUP = 4
MOST = 128
TAIL = 16

norm_eps = 1e-06
rope_base = 10000.0
neg_large = -1e30
inv_root = HEAD_SIZE ** (-0.5)

f32 = jnp.float32
bf16 = jnp.bfloat16
PLANE = ("row", "col")


def dot(a, b):
    return lax.dot_general(a, b, (((1,), (0,)), ((), ())), preferred_element_type=f32)


def dot_nt(a, b):
    return lax.dot_general(a, b, (((1,), (1,)), ((), ())), preferred_element_type=f32)


def dot_tn(a, b):
    return lax.dot_general(a, b, (((0,), (0,)), ((), ())), preferred_element_type=f32)


def split_bits(value):
    high = value.astype(bf16)
    return high, (value - high.astype(f32)).astype(bf16)


def iota(shape, dim):
    return lax.broadcasted_iota(jnp.int32, shape, dim)


def params(mib, **more):
    return pltpu.CompilerParams(vmem_limit_bytes=mib * 1024 * 1024, **more)


def hint(micros):
    return pl.CostEstimate(flops=0, bytes_accessed=3_000_000 * micros, transcendentals=0)


def pack_tables(lengths, packed_length):
    seq_ends = jnp.cumsum(lengths, axis=1)
    starts = seq_ends - lengths
    places = jnp.arange(packed_length, dtype=jnp.int32)
    segment = jnp.sum((places[None, :, None] >= seq_ends[:, None, :]).astype(jnp.int32), axis=2)
    labels = jnp.arange(lengths.shape[1], dtype=jnp.int32)
    seq_start = jnp.sum(
        jnp.where(segment[:, :, None] == labels[None, None, :], starts[:, None, :], 0), axis=2
    )
    return (segment, places[None, :] - seq_start)


def swap_halves(value):
    lane = iota(value.shape, 1) % HEAD_SIZE
    width = value.shape[1]
    return jnp.where(
        lane < HEAD_SIZE // 2,
        pltpu.roll(value, width - HEAD_SIZE // 2, 1),
        pltpu.roll(value, HEAD_SIZE // 2, 1),
    )


def fold(value):
    return value + pltpu.roll(value, HEAD_SIZE, 1)


def twice(pair):
    rolled = pltpu.roll(pair, HEAD_SIZE, 1)
    first = iota(pair.shape, 1) < HEAD_SIZE
    return jnp.where(first, pair, rolled).astype(bf16), jnp.where(first, rolled, pair).astype(bf16)


def block_mask(seg_rows, seg_cols, offset, size, limit):
    same = seg_rows[offset : offset + size] == seg_cols[:, :limit]
    rows = iota((size, limit), 0) + offset
    return same & (rows >= iota((size, limit), 1))


Q_BLOCK = 256


def attn_fwd_kernel(place_ref, *refs):
    part_refs, refs = refs[:8], refs[8:]
    w_ref, cos_ref, sin_ref, segr_ref, segc_ref, x_ref, qkv_ref, out_ref, lse_ref, joined_ref = refs
    rows = part_refs[0].shape[1]
    packed = 8 * rows
    for index, part_ref in enumerate(part_refs):
        at = pl.ds(pl.multiple_of(place_ref[index] * rows, rows), rows)
        part = part_ref[0]
        x_ref[0, at] = part
        joined_ref[at] = dot(part, w_ref[...])
    joined = joined_ref[...]
    cosine, sine = cos_ref[0], sin_ref[0]
    first = iota((packed, 128), 1) < HEAD_SIZE
    query = joined[:, :128]
    pair = joined[:, 128:]
    query = query * cosine + swap_halves(query) * sine
    pair = jnp.where(first, pair * cosine + swap_halves(pair) * sine, pair)
    query = query.astype(bf16)
    pair16 = pair.astype(bf16)
    qkv_ref[0, :, :128] = query
    qkv_ref[0, :, 128:] = pair16
    keys, values = twice(pair16.astype(f32))
    seg_rows, seg_cols = segr_ref[0], segc_ref[0]
    lane = iota((Q_BLOCK, 128), 1)
    for offset in range(0, packed, Q_BLOCK):
        limit = offset + Q_BLOCK
        mask = block_mask(seg_rows, seg_cols, offset, Q_BLOCK, limit)
        outs, sums = [], []
        for head in range(2):
            mine = (lane < HEAD_SIZE) if head == 0 else (lane >= HEAD_SIZE)
            rows_q = jnp.where(mine, query[offset:limit], jnp.zeros((), bf16))
            scores = dot_nt(rows_q, keys[:limit]) * inv_root
            scores = jnp.where(mask, scores, neg_large)
            top = jnp.max(scores, axis=1, keepdims=True)
            part = jnp.exp(scores - top)
            total = jnp.sum(part, axis=1, keepdims=True)
            weights = (part * (1.0 / total)).astype(bf16)
            outs.append(dot(weights, values[:limit]))
            sums.append(top + jnp.log(total))
        merged = jnp.where(lane < HEAD_SIZE, outs[0], outs[1]).astype(bf16)
        out_ref[offset // rows : limit // rows, 0] = merged.reshape(Q_BLOCK // rows, rows, 128)
        lse_ref[0, offset:limit] = jnp.where(lane < HEAD_SIZE, sums[0], sums[1])


def attn_bwd_kernel(
    x_ref, w_ref, cos_ref, sin_ref, segr_ref, segc_ref, qkv_ref, lse_ref, grad_ref,
    joined_ref, weight_ref, total_ref, dk_ref, dv_ref,
):
    devices, _, rows, _ = grad_ref.shape
    packed = devices * rows
    m = pl.program_id(0)
    query = qkv_ref[0, :, :128]
    keys, values = twice(qkv_ref[0, :, 128:].astype(f32))
    seg_rows, seg_cols = segr_ref[0], segc_ref[0]
    grad = grad_ref[:, 0].reshape(packed, 128)
    lane = iota((Q_BLOCK, 128), 1)
    zero = jnp.zeros((), bf16)
    dk_ref[...] = jnp.zeros_like(dk_ref)
    dv_ref[...] = jnp.zeros_like(dv_ref)
    grad_query = []
    for offset in range(0, packed, Q_BLOCK):
        limit = offset + Q_BLOCK
        mask = block_mask(seg_rows, seg_cols, offset, Q_BLOCK, limit)
        parts = []
        for head in range(2):
            mine = (lane < HEAD_SIZE) if head == 0 else (lane >= HEAD_SIZE)
            rows_q = jnp.where(mine, query[offset:limit], zero)
            rows_g = jnp.where(mine, grad[offset:limit], zero)
            scores = dot_nt(rows_q, keys[:limit]) * inv_root
            at = head * HEAD_SIZE
            probs = jnp.exp(jnp.where(mask, scores, neg_large) - lse_ref[0, offset:limit, at : at + 1])
            grad_probs = dot_nt(rows_g, values[:limit])
            weighed = probs * grad_probs
            delta = jnp.sum(weighed, axis=1, keepdims=True)
            grad_scores = (weighed - probs * delta).astype(bf16)
            parts.append(dot(grad_scores, keys[:limit]))
            dk_ref[:limit] += dot_tn(grad_scores, rows_q)
            dv_ref[:limit] += dot_tn(probs.astype(bf16), rows_g)
        grad_query.append(jnp.where(lane < HEAD_SIZE, parts[0], parts[1]))
    dq = jnp.concatenate(grad_query, axis=0) * inv_root
    dk = fold(dk_ref[...]) * inv_root
    dv = fold(dv_ref[...])
    cosine, sine = cos_ref[0], sin_ref[0]
    first = iota((packed, 128), 1) < HEAD_SIZE
    dq = dq * cosine - swap_halves(dq) * sine
    dk = dk * cosine - swap_halves(dk) * sine
    joined = jnp.concatenate([dq, jnp.where(first, dk, dv)], axis=1).astype(bf16)
    joined_ref[:, 0] = joined.reshape(devices, rows, 256)
    part = dot_tn(x_ref[0], joined)

    @pl.when(m == 0)
    def _():
        total_ref[...] = part

    @pl.when(m > 0)
    def _():
        total_ref[...] += part

    @pl.when(m == pl.num_programs(0) - 1)
    def _():
        half = weight_ref.shape[1] - TAIL
        high, low = split_bits(total_ref[...] * w_ref[...].astype(f32))
        ones = jnp.ones((8, high.shape[1]), bf16)
        scaled = (dot_nt(ones, high) + dot_nt(ones, low))[:1]
        scaled = jnp.concatenate([scaled[:, i * 256 : (i + 1) * 256] for i in range(4)], axis=0)
        high, low = split_bits(scaled)
        extra = jnp.concatenate(
            [high.astype(f32), low.astype(f32), jnp.zeros((TAIL - 8, 256), f32)], axis=0
        ).astype(bf16)
        for h in range(2):
            weight_ref[h, :half] = total_ref[h * half : (h + 1) * half].astype(bf16)
            weight_ref[h, half:] = extra


def wide_of_dense(dense):
    return jnp.concatenate([dense[8 * b : 8 * b + 8] for b in range(EXPERTS // 8)], axis=1)


def dense_of_wide(wide):
    part = wide.shape[1] // (EXPERTS // 8)
    return jnp.concatenate(
        [wide[:, b * part : (b + 1) * part] for b in range(EXPERTS // 8)], axis=0
    )


def token_fwd_kernel(place_ref, *refs):
    w_refs, refs = refs[:8], refs[8:]
    heads_ref, x_ref, gain_ref, router_ref, rank_ref, mixed_ref, send_ref, gates_ref = refs
    mixed = x_ref[...]
    for index, w_ref in enumerate(w_refs):
        mixed = mixed + dot(heads_ref[place_ref[index]], w_ref[...])
    mixed_ref[...] = mixed
    scale = lax.rsqrt(jnp.mean(mixed * mixed, axis=1, keepdims=True) + norm_eps)
    normed = (mixed * scale * gain_ref[...]).astype(bf16)
    rows = normed.shape[0]
    send_ref[:rows] = normed
    logits = dot_nt(router_ref[...], normed)
    used = rank_ref[...].astype(f32) >= 0
    logits = jnp.where(used, logits, neg_large)
    part = jnp.where(used, jnp.exp(logits - jnp.max(logits, axis=0, keepdims=True)), 0.0)
    gates = part / jnp.sum(part, axis=0, keepdims=True)
    gates_ref[...] = gates
    high, low = split_bits(wide_of_dense(gates))
    send_ref[rows:] = jnp.concatenate([high.astype(f32), low.astype(f32)], axis=0).astype(bf16)


def token_bwd_kernel(place_ref, *refs):
    w_refs, refs = refs[:8], refs[8:]
    (
        back_ref, mixed_ref, out_grad_ref, gates_ref, heads_ref, gain_ref, router_ref, normed_ref,
        grad_mixed_ref, grad_heads_ref, sums_ref,
    ) = refs
    rows = mixed_ref.shape[0]
    tail = back_ref[rows:].astype(f32)
    grad_gates = dense_of_wide(tail[:8] + tail[8:])
    gates = gates_ref[...]
    weighed = gates * grad_gates
    spread = weighed - gates * jnp.sum(weighed, axis=0, keepdims=True)
    high, low = split_bits(spread)
    router = router_ref[...]
    grad_normed = back_ref[:rows].astype(f32) + dot_tn(high, router) + dot_tn(low, router)
    normed = normed_ref[:rows]
    router_grad = dot(high, normed) + dot(low, normed)
    mixed = mixed_ref[...]
    scale = lax.rsqrt(jnp.mean(mixed * mixed, axis=1, keepdims=True) + norm_eps)
    lifted = grad_normed * gain_ref[...]
    gain_grad = jnp.sum(grad_normed * mixed * scale, axis=0, keepdims=True)
    inner = jnp.mean(lifted * mixed, axis=1, keepdims=True)
    grad_mixed = out_grad_ref[...] + scale * lifted - mixed * (scale * scale * scale * inner)
    grad_mixed_ref[...] = grad_mixed
    branch = grad_mixed.astype(bf16)
    for index, w_ref in enumerate(w_refs):
        grad_heads_ref[place_ref[index]] = dot_nt(branch, w_ref[...]).astype(bf16)
    count = heads_ref.shape[0]
    for j in range(count):
        sums_ref[j, :128] = dot_tn(heads_ref[j], branch).astype(bf16)
        part = router_grad[j * (EXPERTS // count) : (j + 1) * (EXPERTS // count)]
        rest = jnp.zeros((TAIL - part.shape[0] - 1, part.shape[1]), f32)
        sums_ref[j, 128:] = jnp.concatenate(
            [part, gain_grad if j == 0 else jnp.zeros_like(gain_grad), rest], axis=0
        ).astype(bf16)


def token_end_kernel(place_ref, *refs):
    w_refs, refs = refs[:8], refs[8:]
    joined_ref, x_ref, gain_ref, grad_mixed_ref, out_ref = refs
    x = x_ref[...]
    total = jnp.zeros_like(x)
    for index, w_ref in enumerate(w_refs):
        total = total + dot_nt(joined_ref[place_ref[index]], w_ref[...])
    scale = lax.rsqrt(jnp.mean(x * x, axis=1, keepdims=True) + norm_eps)
    lifted = total * gain_ref[...]
    inner = jnp.mean(lifted * x, axis=1, keepdims=True)
    out_ref[...] = grad_mixed_ref[...] + scale * lifted - x * (scale * scale * scale * inner)


def expert_kernel(sides, steps, base_ref, bits_ref, *refs):
    token_refs, refs = refs[: 2 * sides], refs[2 * sides :]
    w_in_ref, w_out_ref, refs = refs[0], refs[1], refs[2:]
    out_refs, refs = refs[:sides], refs[sides:]
    back_refs, refs = (refs[:1], *(refs[i : i + 2] for i in range(1, 2 * sides - 1, 2))), refs[2 * sides - 1 :]
    send_refs, keep_refs, refs = refs[:steps], refs[steps : 2 * steps], refs[2 * steps :]
    x_scr, g_scr, gate_scr, rank_scr, out_acc, back_acc, gg_acc, sum_acc = refs
    group, step = pl.program_id(0), pl.program_id(1)
    chosen = base_ref[0] + step
    tokens = token_refs[0].shape[1] - TAIL

    @pl.when(step == 0)
    def _():
        out_acc[...] = jnp.zeros_like(out_acc)
        back_acc[...] = jnp.zeros_like(back_acc)
        gg_acc[...] = jnp.zeros_like(gg_acc)

    blocks = EXPERTS // 8

    def matches(s):
        return iota((MOST, tokens), 0) == rank_scr[s : s + 1].astype(jnp.int32)

    def bring(rows_ref, grads_ref):
        for s in range(GROUP):
            wide = rows_ref[s, tokens:].astype(f32)
            wide = wide[:8] + wide[8:]
            ranks = grads_ref[s, tokens:].astype(f32)[:8]
            gate_row = jnp.zeros((1, tokens), f32)
            rank_row = jnp.zeros((1, tokens), f32)
            for b in range(blocks):
                lanes = slice(b * tokens, (b + 1) * tokens)
                mine = iota((8, tokens), 0) + 8 * b == chosen
                gate_row += jnp.sum(jnp.where(mine, wide[:, lanes], 0.0), axis=0, keepdims=True)
                rank_row += jnp.sum(jnp.where(mine, ranks[:, lanes], 0.0), axis=0, keepdims=True)
            rank_scr[s : s + 1] = rank_row
            hit = iota((MOST, tokens), 0) == rank_row.astype(jnp.int32)
            spot = jnp.where(hit, 1.0, 0.0).astype(bf16)
            at = slice(s * MOST, (s + 1) * MOST)
            x_scr[at] = dot(spot, rows_ref[s, :tokens]).astype(bf16)
            g_scr[at] = dot(spot, grads_ref[s, :tokens]).astype(bf16)
            gate_scr[at] = jnp.sum(jnp.where(hit, gate_row, 0.0), axis=1, keepdims=True)

    if sides == 1:
        bring(*token_refs)
    else:
        for side in range(sides):
            pl.when(group == side)(functools.partial(bring, *token_refs[2 * side : 2 * side + 2]))

    x, g, gate = x_scr[...], g_scr[...], gate_scr[...]
    act = dot(x, w_in_ref[0])
    gate_part, up_part = act[:, :FF], act[:, FF:]
    sig = jax.nn.sigmoid(gate_part)
    silu = gate_part * sig
    hidden = silu * up_part
    raw = dot_nt(g, w_out_ref[0])
    grad_gates = jnp.sum(hidden * raw, axis=1, keepdims=True)
    scaled = (hidden * gate).astype(bf16)
    produced = dot(scaled, w_out_ref[0]).astype(bf16)
    grad_hidden = raw * gate
    grad_act = jnp.concatenate(
        [grad_hidden * up_part * sig * (1.0 + gate_part * (1.0 - sig)), grad_hidden * silu], axis=1
    ).astype(bf16)
    grad_rows = dot_nt(grad_act, w_in_ref[0]).astype(bf16)

    tall, low = x.shape[1] // 2, FF // 2
    half = tall + low

    @pl.when(group == 0)
    def _():
        sum_acc[step] = jnp.zeros(sum_acc.shape[1:], f32)

    for h in range(2):
        sum_acc[step, h * half : h * half + tall] += dot_tn(
            x_scr[:, h * tall : (h + 1) * tall], grad_act
        )
        sum_acc[step, h * half + tall : (h + 1) * half] += dot_tn(
            scaled[:, h * low : (h + 1) * low], g_scr[...]
        )

    for index in range(steps):

        @pl.when((group == pl.num_programs(0) - 1) & (step == index))
        def _():
            bit = bits_ref[index]
            other = pl.ds(pl.multiple_of((1 - bit) * half, half), half)
            send_refs[index][...] = sum_acc[index, other].astype(bf16)
            own = pl.ds(pl.multiple_of(bit * half, half), half)
            keep_refs[index][...] = sum_acc[index, own].astype(bf16)

    for s in range(GROUP):
        hit = matches(s)
        spot = jnp.where(hit, 1.0, 0.0).astype(bf16)
        at = slice(s * MOST, (s + 1) * MOST)
        out_acc[s] += dot_tn(spot, produced[at])
        back_acc[s] += dot_tn(spot, grad_rows[at])
        row = jnp.sum(jnp.where(hit, grad_gates[at], 0.0), axis=0, keepdims=True)
        wide = jnp.concatenate([jnp.broadcast_to(row, (8, tokens))] * blocks, axis=1)
        index = iota(wide.shape, 1) // tokens * 8 + iota(wide.shape, 0)
        gg_acc[s] += jnp.where(index == chosen, wide, 0.0)

    for side in range(sides):
        ours = True if sides == 1 else group == side

        @pl.when((step == steps - 1) & ours)
        def _():
            for s in range(GROUP):
                out_refs[side][s] = out_acc[s].astype(bf16)
                each = GROUP // len(back_refs[side])
                back_ref, at = back_refs[side][s // each], s % each
                back_ref[at, :tokens] = back_acc[s].astype(bf16)
                high, low_part = split_bits(gg_acc[s])
                back_ref[at, tokens:] = jnp.concatenate(
                    [high.astype(f32), low_part.astype(f32)], axis=0
                ).astype(bf16)


def run_experts(base, begin, bits, sides, w_in, w_out, steps):
    sources, full, width = sides[0][0].shape
    tokens = full - TAIL
    count = len(sides)
    groups = count if count > 1 else sources // GROUP
    half = (width + FF) // 2
    by_group = (lambda g, e, *_: (0, 0, 0)) if count > 1 else (lambda g, e, *_: (g, 0, 0))
    by_expert = lambda g, e, base, bits, begin: (begin[0] + e, 0, 0)

    def kernel(base_ref, bits_ref, begin_ref, *refs):
        expert_kernel(count, steps, base_ref, bits_ref, *refs)

    single = pl.Buffered(1)
    tokens_mode = single if count > 1 else None
    half_spec = pl.BlockSpec((half, width), lambda g, e, *_: (0, 0), pipeline_mode=single)
    results = pl.pallas_call(
        kernel,
        grid_spec=pltpu.PrefetchScalarGridSpec(
            num_scalar_prefetch=3,
            grid=(groups, steps),
            in_specs=[
                *[pl.BlockSpec((GROUP, full, width), by_group, pipeline_mode=tokens_mode)]
                * (2 * count),
                pl.BlockSpec((1, width, 2 * FF), by_expert),
                pl.BlockSpec((1, FF, width), by_expert),
            ],
            out_specs=[
                *[pl.BlockSpec((GROUP, tokens, width), by_group, pipeline_mode=single)] * count,
                pl.BlockSpec((GROUP, full, width), by_group, pipeline_mode=single),
                *[pl.BlockSpec((GROUP // 2, full, width), by_group, pipeline_mode=single)]
                * (2 * count - 2),
                *[half_spec] * (2 * steps),
            ],
            scratch_shapes=[
                pltpu.VMEM((GROUP * MOST, width), bf16),
                pltpu.VMEM((GROUP * MOST, width), bf16),
                pltpu.VMEM((GROUP * MOST, 1), f32),
                pltpu.VMEM((8, tokens), f32),
                pltpu.VMEM((GROUP, tokens, width), f32),
                pltpu.VMEM((GROUP, tokens, width), f32),
                pltpu.VMEM((GROUP, 8, width), f32),
                pltpu.VMEM((steps, 2 * half, width), f32),
            ],
        ),
        out_shape=[
            *[jax.ShapeDtypeStruct((sources, tokens, width), bf16)] * count,
            jax.ShapeDtypeStruct((sources, full, width), bf16),
            *[jax.ShapeDtypeStruct((GROUP // 2, full, width), bf16)] * (2 * count - 2),
            *[jax.ShapeDtypeStruct((half, width), bf16)] * (2 * steps),
        ],
        compiler_params=params(62),
        cost_estimate=pl.CostEstimate(
            flops=steps * groups * 512 * 9_400_000, bytes_accessed=30_000_000, transcendentals=0
        ),
        name="experts",
    )(base.reshape(1), bits, begin.reshape(1), *[v for side in sides for v in side], w_in, w_out)
    outs, results = results[:count], results[count:]
    backs, results = results[: 2 * count - 1], results[2 * count - 1 :]
    return outs, backs, results[:steps], results[steps:]


def sum_backs_kernel(*refs):
    own, rest, out_ref = refs[:2], refs[2:6], refs[6]
    total = own[0][...].astype(f32) + own[1][...].astype(f32)
    early = rest[0][...].astype(f32) + rest[2][...].astype(f32)
    late = rest[1][...].astype(f32) + rest[3][...].astype(f32)
    out_ref[...] = (total + jnp.where(pl.program_id(0) < GROUP // 2, early, late)).astype(bf16)


def sum_backs(own, came):
    _, full, width = own[0].shape
    spec = lambda index: pl.BlockSpec((1, full, width), lambda i: (index(i), 0, 0))
    first = spec(lambda i: jnp.minimum(i, GROUP // 2 - 1))
    second = spec(lambda i: jnp.maximum(i - GROUP // 2, 0))
    return pl.pallas_call(
        sum_backs_kernel,
        grid=(GROUP,),
        in_specs=[spec(lambda i: i)] * 2 + [first, second] * 2,
        out_specs=spec(lambda i: i),
        out_shape=jax.ShapeDtypeStruct((GROUP, full, width), bf16),
        compiler_params=params(32),
        name="sum_backs",
    )(*own, *came)


def trade(value, axis, bit):
    size = lax.axis_size(axis)
    return lax.ppermute(value, axis, [(i, i ^ bit) for i in range(size)])


def pick(value, index):
    return lax.dynamic_index_in_dim(value, index, axis=0, keepdims=False)


def after(value, *others):
    return lax.optimization_barrier((value, *others))[0]


def add_split_kernel(bit_ref, keep_other, came_other, keep_own, came_own, send_ref, own_ref):
    send_ref[...] = (keep_other[...].astype(f32) + came_other[...].astype(f32)).astype(bf16)
    own_ref[...] = (keep_own[...].astype(f32) + came_own[...].astype(f32)).astype(bf16)


def add_split(bit, keep, came):
    rows, width = came.shape
    tile = 128
    tiles = rows // 2 // tile
    other = pl.BlockSpec((tile, width), lambda i, bit: ((1 - bit[0]) * tiles + i, 0))
    own = pl.BlockSpec((tile, width), lambda i, bit: (bit[0] * tiles + i, 0))
    result = pl.BlockSpec((tile, width), lambda i, bit: (i, 0))
    return pl.pallas_call(
        add_split_kernel,
        grid_spec=pltpu.PrefetchScalarGridSpec(
            num_scalar_prefetch=1,
            grid=(tiles,),
            in_specs=[other, other, own, own],
            out_specs=[result, result],
        ),
        out_shape=[jax.ShapeDtypeStruct((rows // 2, width), bf16)] * 2,
        cost_estimate=hint(16),
        name="add_split",
    )(bit.reshape(1), keep, came, keep, came)


def add_pairs_kernel(a_ref, b_ref, c_ref, d_ref, out_ref):
    out_ref[0] = (a_ref[...].astype(f32) + b_ref[...].astype(f32)).astype(bf16)
    out_ref[1] = (c_ref[...].astype(f32) + d_ref[...].astype(f32)).astype(bf16)


def add_pairs(a, b, c, d):
    rows, width = a.shape
    tile = 128
    return pl.pallas_call(
        add_pairs_kernel,
        grid=(rows // tile,),
        in_specs=[pl.BlockSpec((tile, width), lambda i: (i, 0))] * 4,
        out_specs=pl.BlockSpec((2, tile, width), lambda i: (0, i, 0)),
        out_shape=jax.ShapeDtypeStruct((2, rows, width), bf16),
        cost_estimate=hint(16),
        name="add_pairs",
    )(a, b, c, d)


def place_kernel(scalars, *refs):
    fronts, fars, gin_ref, gout_ref = refs[:3], refs[3:5], refs[-2], refs[-1]
    quarter_rows = fronts[0].shape[1]
    for path in range(2):
        for k in range(4):
            value = (fronts[k][path] if k < 3 else fars[path][...]).astype(f32)
            half, quarter = scalars[1 + path * 8 + 2 * k], scalars[2 + path * 8 + 2 * k]

            @pl.when(quarter == 0)
            def _():
                at = pl.ds(pl.multiple_of(half * FF, FF), quarter_rows)
                gin_ref[path, at] = value

            @pl.when(quarter == 1)
            def _():
                at = pl.ds(pl.multiple_of(half * FF, FF) + quarter_rows, FF - quarter_rows)
                gin_ref[path, at] = value[: FF - quarter_rows]
                at = pl.ds(pl.multiple_of(half * (FF // 2), FF // 2), FF // 2)
                gout_ref[path, at] = value[FF - quarter_rows :]


def place(block, spots, pieces, experts, before):
    width = pieces[0].shape[-1]
    kept = [] if before is None else list(before)
    lanes = width // 4
    whole = lambda value: pl.BlockSpec(
        (*value.shape[:-1], lanes), lambda i, c: (0,) * (value.ndim - 1) + (i,)
    )
    return pl.pallas_call(
        place_kernel,
        grid_spec=pltpu.PrefetchScalarGridSpec(
            num_scalar_prefetch=1,
            grid=(4,),
            in_specs=[whole(value) for value in pieces]
            + [pl.BlockSpec(memory_space=pl.ANY)] * len(kept),
            out_specs=[
                pl.BlockSpec((2, width, lanes), lambda i, c: (c[0], 0, i)),
                pl.BlockSpec((2, FF, lanes), lambda i, c: (c[0], 0, i)),
            ],
        ),
        out_shape=[
            jax.ShapeDtypeStruct((experts, width, 2 * FF), f32),
            jax.ShapeDtypeStruct((experts, FF, width), f32),
        ],
        input_output_aliases={} if before is None else {6: 0, 7: 1},
        compiler_params=params(58),
        name="place",
    )(jnp.concatenate([block.reshape(1), spots]), *pieces, *kept)


def plane_parts(value, *between):
    half = value.shape[0] // 2
    along, across = trade(value, "row", 1), trade(value, "row", 2)
    there = trade(value, "col", 1)
    along, across = after((along, across), *between)
    far = jnp.concatenate(
        [trade(along[:half], "row", 2), trade(across[half:], "row", 1)], axis=0
    )
    return [value, along, across, far, there] + [
        trade(part, "col", 1) for part in (along, across, far)
    ]


def dp_send(value):
    if lax.axis_size("dp") != 4:
        return (lax.psum(value, "dp"),)
    return (value, *[trade(value, "dp", k) for k in range(1, 4)])


def body(
    block_input,
    seq_lengths,
    routes,
    norm1_gain,
    w_qkv,
    w_heads,
    norm2_gain,
    router,
    w_expert_in,
    w_expert_out,
    out_grad,
):
    tok_rows, batches, width = block_input.shape
    dp_size = lax.axis_size("dp")
    plane = lax.axis_size("row") * lax.axis_size("col")
    packed = tok_rows * plane
    tokens = tok_rows * batches
    dp_at = lax.axis_index("dp").astype(jnp.int32)
    sds = jax.ShapeDtypeStruct

    x = jnp.transpose(block_input, (1, 0, 2)).reshape(tokens, width)
    og = jnp.transpose(out_grad, (1, 0, 2)).reshape(tokens, width)
    scale1 = lax.rsqrt(jnp.mean(x * x, axis=1, keepdims=True) + norm_eps)
    normed1 = (x * scale1 * norm1_gain).astype(bf16)
    flat_routes = jnp.transpose(routes, (1, 0, 2)).reshape(tokens, -1)
    used = jnp.any(
        flat_routes[None] == jnp.arange(EXPERTS, dtype=jnp.int32)[:, None, None], axis=2
    )
    before = (
        jnp.arange(tokens, dtype=jnp.int32)[:, None] < jnp.arange(tokens, dtype=jnp.int32)[None, :]
    )
    counted = jnp.dot(used.astype(bf16), before.astype(bf16), preferred_element_type=f32)
    rank = jnp.where(used, counted, -1.0).astype(bf16)
    rank_rows = jnp.transpose(rank.reshape(EXPERTS // 8, 8, tokens), (1, 0, 2)).reshape(8, -1)
    grads_in = lax.all_gather(
        jnp.concatenate([og.astype(bf16), rank_rows, jnp.zeros_like(rank_rows)], axis=0),
        "dp",
        axis=0,
        tiled=False,
    )

    segment, position = pack_tables(seq_lengths[0], packed)
    inverse = jnp.exp(
        -(2.0 * jnp.arange(HEAD_SIZE // 2, dtype=f32) / HEAD_SIZE) * math.log(rope_base)
    )
    angles = position.astype(f32)[:, :, None] * inverse[None, None, :]
    cosine, sine = jnp.cos(angles), jnp.sin(angles)
    cosine = jnp.concatenate([cosine] * 4, axis=2)
    sine = jnp.concatenate([-sine, sine, -sine, sine], axis=2)
    seg_rows, seg_cols = segment[:, :, None], segment[:, None, :]

    row = lax.axis_index("row").astype(jnp.int32)
    col = lax.axis_index("col").astype(jnp.int32)
    places = jnp.stack([(row ^ k) * 2 + (col ^ c) for c in range(2) for k in range(4)])
    w_group = lax.all_to_all(w_qkv, "col", split_axis=1, concat_axis=0, tiled=True)
    parts = plane_parts(
        normed1.reshape(batches, tok_rows, width), cosine, sine, seg_rows, seg_cols, w_group
    )

    per_m = lambda m, *_: (m, 0, 0)
    const = lambda m, *_: (0, 0)
    by_device = lambda m, *_: (0, m, 0, 0)
    table_specs = [
        pl.BlockSpec((1, packed, 128), per_m),
        pl.BlockSpec((1, packed, 128), per_m),
        pl.BlockSpec((1, packed, 1), per_m),
        pl.BlockSpec((1, 1, packed), per_m),
    ]
    x_all, qkv, head_out, lse = pl.pallas_call(
        attn_fwd_kernel,
        grid_spec=pltpu.PrefetchScalarGridSpec(
            num_scalar_prefetch=1,
            grid=(batches,),
            in_specs=[
                *[pl.BlockSpec((1, tok_rows, width), per_m)] * 8,
                pl.BlockSpec((width, 256), const),
                *table_specs,
            ],
            out_specs=[
                pl.BlockSpec((1, packed, width), per_m),
                pl.BlockSpec((1, packed, 256), per_m),
                pl.BlockSpec((plane, 1, tok_rows, 128), by_device),
                pl.BlockSpec((1, packed, 128), per_m),
            ],
            scratch_shapes=[pltpu.VMEM((packed, 256), f32)],
        ),
        out_shape=[
            sds((batches, packed, width), bf16),
            sds((batches, packed, 256), bf16),
            sds((plane, batches, tok_rows, 128), bf16),
            sds((batches, packed, 128), f32),
        ],
        compiler_params=params(48),
        name="attn_fwd",
    )(places, *parts, w_group, cosine, sine, seg_rows, seg_cols)

    heads = lax.all_to_all(
        head_out.reshape(plane, tokens, 128), PLANE, split_axis=0, concat_axis=0, tiled=True
    )
    gain1, gain2 = norm1_gain.reshape(1, width), norm2_gain.reshape(1, width)
    router_t = jnp.transpose(router)
    w_heads_parts = plane_parts(after(w_heads, parts[3]), head_out)

    def with_places(kernel, count, outs, mib, name):
        in_vmem = pl.BlockSpec(memory_space=pltpu.VMEM)
        return pl.pallas_call(
            kernel,
            in_specs=[pl.BlockSpec(memory_space=pltpu.SMEM)] + [in_vmem] * count,
            out_shape=outs,
            compiler_params=params(mib),
            name=name,
        )

    mixed, send, gates = with_places(
        token_fwd_kernel,
        13,
        [
            sds((tokens, width), f32),
            sds((tokens + TAIL, width), bf16),
            sds((EXPERTS, tokens), f32),
        ],
        32,
        "token_fwd",
    )(places, *w_heads_parts, heads, x, gain2, router_t, rank)

    rows_in = lax.all_gather(send, "dp", axis=0, tiled=False)
    w_group_parts = plane_parts(after(w_group, send))
    here = w_expert_in.shape[0]
    first, second = row % 2, (row // 2) % 2
    bits = jnp.stack([first, second])
    shared = here == 8
    chunks = []
    if shared:
        grads_there = trade(grads_in, "col", 1)
        rows_in = after(rows_in, w_group_parts, grads_there)
        rows_there = trade(rows_in, "col", 1)
        own_backs, came_backs, outs = [], [], []
        for index in range(2):
            begin = 4 * col + 2 * index
            out, back, away, kept = run_experts(
                dp_at * here + begin,
                begin,
                bits,
                ((rows_in, grads_in), (rows_there, grads_there)),
                w_expert_in,
                w_expert_out,
                2,
            )
            own_backs.append(back[0])
            came_backs += [trade(value, "col", 1) for value in back[1:]]
            outs += [out[0], trade(out[1], "col", 1)]
            chunks.append((away, kept))
            rows_there = after(rows_there, back[0])
            last = back[0]
    else:
        zero = jnp.zeros_like(dp_at)
        outs, (back,), away, kept = run_experts(
            dp_at * here,
            zero,
            jnp.zeros_like(bits),
            ((rows_in, grads_in),),
            w_expert_in,
            w_expert_out,
            1,
        )

    flips = (1, 2)
    halves = []

    def first_sum(away, kept, *order):
        kept = after(kept, *order)
        came = [trade(away[path], "row", flips[path]) for path in range(2)]
        return [add_split(bits[1 - path], kept[path], came[path]) for path in range(2)]

    def second_sum(halves, *order):
        came = [trade(halves[path][0], "row", flips[1 - path]) for path in range(2)]
        own = after((halves[0][1], halves[1][1]), *order)
        return add_pairs(own[0], came[0], own[1], came[1])

    if shared:
        halves.append(first_sum(*chunks[0], last))
        own_backs = after(own_backs, halves[0])
        back = sum_backs(own_backs, came_backs)
        halves.append(first_sum(*chunks[1], back))
        ready_a = second_sum(halves[0], halves[1])
    back = lax.psum_scatter(
        back.reshape(dp_size * (tokens + TAIL), width), "dp", scatter_dimension=0, tiled=True
    )
    if shared:
        back = after(back, ready_a)
    grad_mixed, grad_heads, sums = with_places(
        token_bwd_kernel,
        16,
        [
            sds((tokens, width), f32),
            sds((plane, tokens, 128), bf16),
            sds((plane, 128 + TAIL, width), bf16),
        ],
        40,
        "token_bwd",
    )(places, *w_heads_parts, back, mixed, og, gates, heads, gain2, router_t, send)
    sums = lax.psum_scatter(
        sums.reshape(plane * (128 + TAIL), width), PLANE, scatter_dimension=0, tiled=True
    )
    outs = after(outs, grad_mixed)
    produced = sum(value.astype(f32) for value in outs).astype(bf16)
    produced = lax.psum_scatter(
        produced.reshape(dp_size * tokens, width), "dp", scatter_dimension=0, tiled=True
    )
    block_output = mixed + produced.astype(f32)

    grad_heads = lax.all_to_all(grad_heads, PLANE, split_axis=0, concat_axis=0, tiled=True)

    def go_round(mine, *order):
        along, across = trade(mine, "row", 1), trade(mine, "row", 2)
        along, across = after((along, across), *order)
        fars = (across[0], along[1])
        return (mine, along, across), fars

    grad_joined, grad_w_qkv = pl.pallas_call(
        attn_bwd_kernel,
        grid=(batches,),
        in_specs=[
            pl.BlockSpec((1, packed, width), per_m),
            pl.BlockSpec((width, 256), const),
            *table_specs,
            pl.BlockSpec((1, packed, 256), per_m),
            pl.BlockSpec((1, packed, 128), per_m),
            pl.BlockSpec((plane, 1, tok_rows, 128), by_device),
        ],
        out_specs=[
            pl.BlockSpec((plane, 1, tok_rows, 256), by_device),
            pl.BlockSpec((2, width // 2 + TAIL, 256), lambda m: (0, 0, 0)),
        ],
        out_shape=[
            sds((plane, batches, tok_rows, 256), bf16),
            sds((2, width // 2 + TAIL, 256), bf16),
        ],
        scratch_shapes=[
            pltpu.VMEM((width, 256), f32),
            pltpu.VMEM((packed, 128), f32),
            pltpu.VMEM((packed, 128), f32),
        ],
        compiler_params=params(48),
        name="attn_bwd",
    )(
        x_all, w_group, cosine, sine, seg_rows, seg_cols, qkv, lse,
        grad_heads.reshape(plane, batches, tok_rows, 128),
    )

    grad_w_qkv = lax.all_to_all(grad_w_qkv, "col", split_axis=0, concat_axis=0, tiled=True)
    qkv_parts = dp_send(grad_w_qkv)
    grad_joined = lax.all_to_all(
        grad_joined.reshape(plane, tokens, 256), PLANE, split_axis=0, concat_axis=0, tiled=True
    )
    if shared:
        ready_b = second_sum(halves[1], grad_joined)
        front_a, fars_a = go_round(after(ready_a, grad_heads), ready_b)
        front_b, fars_b = go_round(ready_b, fars_a)
    input_grad = with_places(token_end_kernel, 12, sds((tokens, width), f32), 32, "token_end")(
        places, *w_group_parts, grad_joined, x, gain1, grad_mixed
    )

    sums = lax.psum(sums, "dp").astype(f32)
    heads_grad = sums[:128]
    half = width // 2
    if shared:
        qkv_parts = after(qkv_parts, fars_b, input_grad)
    qkv_sums = sum(value.astype(f32) for value in qkv_parts)
    grad_w_qkv = jnp.concatenate([qkv_sums[0, :half], qkv_sums[1, :half]], axis=1)
    scaled = qkv_sums[:, half : half + 4] + qkv_sums[:, half + 4 : half + 8]
    scaled = jnp.sum(scaled, axis=0).reshape(1, width)
    rest = lax.all_gather(
        jnp.concatenate([scaled, sums[128:], jnp.zeros((7, width), f32)], axis=0),
        PLANE,
        axis=0,
        tiled=False,
    )
    per = EXPERTS // plane
    norm1_grad = jnp.sum(rest[::2, 0], axis=0) / norm1_gain
    router_grad = jnp.transpose(rest[:, 1 : 1 + per].reshape(EXPERTS, width))
    norm2_grad = rest[0, 1 + per]

    if shared:
        grad_experts = None
        order = ((), (input_grad, norm1_grad, router_grad, heads_grad, grad_w_qkv, block_output))
        for index, (front, fars) in enumerate(((front_a, fars_a), (front_b, fars_b))):
            pieces = (*front, trade(fars[0], "row", 1), trade(fars[1], "row", 2))
            there = tuple(trade(value, "col", 1) for value in pieces)
            pieces = after(pieces, *order[index])
            spots = []
            for path in range(2):
                for k in range(4):
                    pair = (first ^ (k & 1), second ^ (k >> 1))
                    spots += [pair[path], pair[1 - path]]
            spots = jnp.stack(spots)
            for owner, values in ((col, pieces), (1 - col, there)):
                grad_experts = place(2 * owner + index, spots, values, here, grad_experts)
        grad_w_in, grad_w_out = grad_experts
    else:
        total = lax.psum(jnp.stack([kept[0], away[0]]), PLANE).astype(f32)
        total = total.reshape(here, 2, (width + FF) // 2, width)
        grad_w_in = total[:, :, : width // 2].reshape(here, width, 2 * FF)
        grad_w_out = total[:, :, width // 2 :].reshape(here, FF, width)

    def placed(value):
        return jnp.transpose(value.reshape(batches, tok_rows, width), (1, 0, 2))

    return (
        placed(block_output),
        placed(input_grad),
        norm1_grad,
        grad_w_qkv,
        heads_grad,
        norm2_grad,
        router_grad,
        grad_w_in,
        grad_w_out,
    )


def solution(mesh):
    return jax.shard_map(
        body,
        mesh=mesh,
        in_specs=(
            P(("dp", "row", "col"), None, None),
            P("dp", None, None),
            P(("dp", "row", "col"), None, None),
            P(),
            P("col", "row"),
            P(("row", "col"), None),
            P(),
            P(),
            P("dp", None, None),
            P("dp", None, None),
            P(("dp", "row", "col"), None, None),
        ),
        out_specs=(
            P(("dp", "row", "col"), None, None),
            P(("dp", "row", "col"), None, None),
            P(),
            P("col", "row"),
            P(("row", "col"), None),
            P(),
            P(),
            P("dp", None, None),
            P("dp", None, None),
        ),
        check_vma=False,
    )
```

```python
import functools
import math

import jax
import jax.numpy as jnp
from jax import lax
from jax.experimental import pallas as pl
from jax.experimental.pallas import tpu as pltpu
from jax.sharding import PartitionSpec as P

HEAD_SIZE = 64
EXPERTS = 32
FF = 512
WIDTH = 1024
GROUP = 4
MOST = 128
TAIL = 16

norm_eps = 1e-06
rope_base = 10000.0
neg_large = -1e30
inv_root = HEAD_SIZE ** (-0.5)

f32 = jnp.float32
bf16 = jnp.bfloat16
PLANE = ("row", "col")


def dot(a, b):
    return lax.dot_general(a, b, (((1,), (0,)), ((), ())), preferred_element_type=f32)


def dot_nt(a, b):
    return lax.dot_general(a, b, (((1,), (1,)), ((), ())), preferred_element_type=f32)


def dot_tn(a, b):
    return lax.dot_general(a, b, (((0,), (0,)), ((), ())), preferred_element_type=f32)


def split_bits(value):
    high = value.astype(bf16)
    return high, (value - high.astype(f32)).astype(bf16)


def iota(shape, dim):
    return lax.broadcasted_iota(jnp.int32, shape, dim)


def params(mib, **more):
    return pltpu.CompilerParams(vmem_limit_bytes=mib * 1024 * 1024, **more)


def hint(micros):
    return pl.CostEstimate(flops=1_000_000_000 * micros, bytes_accessed=0, transcendentals=0)


def pack_tables(lengths, packed_length):
    seq_ends = jnp.cumsum(lengths, axis=1)
    starts = seq_ends - lengths
    places = jnp.arange(packed_length, dtype=jnp.int32)
    segment = jnp.sum((places[None, :, None] >= seq_ends[:, None, :]).astype(jnp.int32), axis=2)
    labels = jnp.arange(lengths.shape[1], dtype=jnp.int32)
    seq_start = jnp.sum(
        jnp.where(segment[:, :, None] == labels[None, None, :], starts[:, None, :], 0), axis=2
    )
    return (segment, places[None, :] - seq_start)


def swap_halves(value):
    lane = iota(value.shape, 1) % HEAD_SIZE
    width = value.shape[1]
    return jnp.where(
        lane < HEAD_SIZE // 2,
        pltpu.roll(value, width - HEAD_SIZE // 2, 1),
        pltpu.roll(value, HEAD_SIZE // 2, 1),
    )


def fold(value):
    return value + pltpu.roll(value, HEAD_SIZE, 1)


def twice(pair):
    rolled = pltpu.roll(pair, HEAD_SIZE, 1)
    first = iota(pair.shape, 1) < HEAD_SIZE
    return jnp.where(first, pair, rolled).astype(bf16), jnp.where(first, rolled, pair).astype(bf16)


def block_mask(seg_rows, seg_cols, offset, size, limit):
    same = seg_rows[offset : offset + size] == seg_cols[:, :limit]
    rows = iota((size, limit), 0) + offset
    return same & (rows >= iota((size, limit), 1))


Q_BLOCK = 256


def attn_fwd_kernel(place_ref, *refs):
    part_refs, refs = refs[:8], refs[8:]
    w_ref, cos_ref, sin_ref, segr_ref, segc_ref, x_ref, qkv_ref, out_ref, lse_ref, joined_ref = refs
    rows = part_refs[0].shape[1]
    packed = 8 * rows
    for index, part_ref in enumerate(part_refs):
        at = pl.ds(pl.multiple_of(place_ref[index] * rows, rows), rows)
        part = part_ref[0]
        x_ref[0, at] = part
        joined_ref[at] = dot(part, w_ref[...])
    joined = joined_ref[...]
    cosine, sine = cos_ref[0], sin_ref[0]
    first = iota((packed, 128), 1) < HEAD_SIZE
    query = joined[:, :128]
    pair = joined[:, 128:]
    query = query * cosine + swap_halves(query) * sine
    pair = jnp.where(first, pair * cosine + swap_halves(pair) * sine, pair)
    query = query.astype(bf16)
    pair16 = pair.astype(bf16)
    qkv_ref[0, :, :128] = query
    qkv_ref[0, :, 128:] = pair16
    keys, values = twice(pair16.astype(f32))
    seg_rows, seg_cols = segr_ref[0], segc_ref[0]
    lane = iota((Q_BLOCK, 128), 1)
    for offset in range(0, packed, Q_BLOCK):
        limit = offset + Q_BLOCK
        mask = block_mask(seg_rows, seg_cols, offset, Q_BLOCK, limit)
        outs, sums = [], []
        for head in range(2):
            mine = (lane < HEAD_SIZE) if head == 0 else (lane >= HEAD_SIZE)
            rows_q = jnp.where(mine, query[offset:limit], jnp.zeros((), bf16))
            scores = dot_nt(rows_q, keys[:limit]) * inv_root
            scores = jnp.where(mask, scores, neg_large)
            top = jnp.max(scores, axis=1, keepdims=True)
            part = jnp.exp(scores - top)
            total = jnp.sum(part, axis=1, keepdims=True)
            weights = (part * (1.0 / total)).astype(bf16)
            outs.append(dot(weights, values[:limit]))
            sums.append(top + jnp.log(total))
        merged = jnp.where(lane < HEAD_SIZE, outs[0], outs[1]).astype(bf16)
        out_ref[offset // rows : limit // rows, 0] = merged.reshape(Q_BLOCK // rows, rows, 128)
        lse_ref[0, offset:limit] = jnp.where(lane < HEAD_SIZE, sums[0], sums[1])


def attn_bwd_kernel(
    x_ref, w_ref, cos_ref, sin_ref, segr_ref, segc_ref, qkv_ref, lse_ref, grad_ref,
    joined_ref, weight_ref, total_ref, dk_ref, dv_ref,
):
    devices, _, rows, _ = grad_ref.shape
    packed = devices * rows
    m = pl.program_id(0)
    query = qkv_ref[0, :, :128]
    keys, values = twice(qkv_ref[0, :, 128:].astype(f32))
    seg_rows, seg_cols = segr_ref[0], segc_ref[0]
    grad = grad_ref[:, 0].reshape(packed, 128)
    lane = iota((Q_BLOCK, 128), 1)
    zero = jnp.zeros((), bf16)
    dk_ref[...] = jnp.zeros_like(dk_ref)
    dv_ref[...] = jnp.zeros_like(dv_ref)
    grad_query = []
    for offset in range(0, packed, Q_BLOCK):
        limit = offset + Q_BLOCK
        mask = block_mask(seg_rows, seg_cols, offset, Q_BLOCK, limit)
        parts = []
        for head in range(2):
            mine = (lane < HEAD_SIZE) if head == 0 else (lane >= HEAD_SIZE)
            rows_q = jnp.where(mine, query[offset:limit], zero)
            rows_g = jnp.where(mine, grad[offset:limit], zero)
            scores = dot_nt(rows_q, keys[:limit]) * inv_root
            at = head * HEAD_SIZE
            probs = jnp.exp(jnp.where(mask, scores, neg_large) - lse_ref[0, offset:limit, at : at + 1])
            grad_probs = dot_nt(rows_g, values[:limit])
            weighed = probs * grad_probs
            delta = jnp.sum(weighed, axis=1, keepdims=True)
            grad_scores = (weighed - probs * delta).astype(bf16)
            parts.append(dot(grad_scores, keys[:limit]))
            dk_ref[:limit] += dot_tn(grad_scores, rows_q)
            dv_ref[:limit] += dot_tn(probs.astype(bf16), rows_g)
        grad_query.append(jnp.where(lane < HEAD_SIZE, parts[0], parts[1]))
    dq = jnp.concatenate(grad_query, axis=0) * inv_root
    dk = fold(dk_ref[...]) * inv_root
    dv = fold(dv_ref[...])
    cosine, sine = cos_ref[0], sin_ref[0]
    first = iota((packed, 128), 1) < HEAD_SIZE
    dq = dq * cosine - swap_halves(dq) * sine
    dk = dk * cosine - swap_halves(dk) * sine
    joined = jnp.concatenate([dq, jnp.where(first, dk, dv)], axis=1).astype(bf16)
    joined_ref[:, 0] = joined.reshape(devices, rows, 256)
    part = dot_tn(x_ref[0], joined)

    @pl.when(m == 0)
    def _():
        total_ref[...] = part

    @pl.when(m > 0)
    def _():
        total_ref[...] += part

    @pl.when(m == pl.num_programs(0) - 1)
    def _():
        half = weight_ref.shape[1] - TAIL
        high, low = split_bits(total_ref[...] * w_ref[...].astype(f32))
        ones = jnp.ones((8, high.shape[1]), bf16)
        scaled = (dot_nt(ones, high) + dot_nt(ones, low))[:1]
        scaled = jnp.concatenate([scaled[:, i * 256 : (i + 1) * 256] for i in range(4)], axis=0)
        high, low = split_bits(scaled)
        extra = jnp.concatenate(
            [high.astype(f32), low.astype(f32), jnp.zeros((TAIL - 8, 256), f32)], axis=0
        ).astype(bf16)
        for h in range(2):
            weight_ref[h, :half] = total_ref[h * half : (h + 1) * half].astype(bf16)
            weight_ref[h, half:] = extra


def wide_of_dense(dense):
    return jnp.concatenate([dense[8 * b : 8 * b + 8] for b in range(EXPERTS // 8)], axis=1)


def dense_of_wide(wide):
    part = wide.shape[1] // (EXPERTS // 8)
    return jnp.concatenate(
        [wide[:, b * part : (b + 1) * part] for b in range(EXPERTS // 8)], axis=0
    )


def token_fwd_kernel(place_ref, *refs):
    w_refs, refs = refs[:8], refs[8:]
    heads_ref, x_ref, gain_ref, router_ref, rank_ref, mixed_ref, send_ref, gates_ref = refs
    mixed = x_ref[...]
    for index, w_ref in enumerate(w_refs):
        mixed = mixed + dot(heads_ref[place_ref[index]], w_ref[...])
    mixed_ref[...] = mixed
    scale = lax.rsqrt(jnp.mean(mixed * mixed, axis=1, keepdims=True) + norm_eps)
    normed = (mixed * scale * gain_ref[...]).astype(bf16)
    rows = normed.shape[0]
    send_ref[:rows] = normed
    logits = dot_nt(router_ref[...], normed)
    used = rank_ref[...].astype(f32) >= 0
    logits = jnp.where(used, logits, neg_large)
    part = jnp.where(used, jnp.exp(logits - jnp.max(logits, axis=0, keepdims=True)), 0.0)
    gates = part / jnp.sum(part, axis=0, keepdims=True)
    gates_ref[...] = gates
    high, low = split_bits(wide_of_dense(gates))
    send_ref[rows:] = jnp.concatenate([high.astype(f32), low.astype(f32)], axis=0).astype(bf16)


def token_bwd_kernel(place_ref, *refs):
    w_refs, refs = refs[:8], refs[8:]
    (
        back_ref, mixed_ref, out_grad_ref, gates_ref, heads_ref, gain_ref, router_ref, normed_ref,
        grad_mixed_ref, grad_heads_ref, sums_ref,
    ) = refs
    rows = mixed_ref.shape[0]
    tail = back_ref[rows:].astype(f32)
    grad_gates = dense_of_wide(tail[:8] + tail[8:])
    gates = gates_ref[...]
    weighed = gates * grad_gates
    spread = weighed - gates * jnp.sum(weighed, axis=0, keepdims=True)
    high, low = split_bits(spread)
    router = router_ref[...]
    grad_normed = back_ref[:rows].astype(f32) + dot_tn(high, router) + dot_tn(low, router)
    normed = normed_ref[:rows]
    router_grad = dot(high, normed) + dot(low, normed)
    mixed = mixed_ref[...]
    scale = lax.rsqrt(jnp.mean(mixed * mixed, axis=1, keepdims=True) + norm_eps)
    lifted = grad_normed * gain_ref[...]
    gain_grad = jnp.sum(grad_normed * mixed * scale, axis=0, keepdims=True)
    inner = jnp.mean(lifted * mixed, axis=1, keepdims=True)
    grad_mixed = out_grad_ref[...] + scale * lifted - mixed * (scale * scale * scale * inner)
    grad_mixed_ref[...] = grad_mixed
    branch = grad_mixed.astype(bf16)
    for index, w_ref in enumerate(w_refs):
        grad_heads_ref[place_ref[index]] = dot_nt(branch, w_ref[...]).astype(bf16)
    count = heads_ref.shape[0]
    for j in range(count):
        sums_ref[j, :128] = dot_tn(heads_ref[j], branch).astype(bf16)
        part = router_grad[j * (EXPERTS // count) : (j + 1) * (EXPERTS // count)]
        rest = jnp.zeros((TAIL - part.shape[0] - 1, part.shape[1]), f32)
        sums_ref[j, 128:] = jnp.concatenate(
            [part, gain_grad if j == 0 else jnp.zeros_like(gain_grad), rest], axis=0
        ).astype(bf16)


def token_end_kernel(place_ref, *refs):
    w_refs, refs = refs[:8], refs[8:]
    joined_ref, x_ref, gain_ref, grad_mixed_ref, out_ref = refs
    x = x_ref[...]
    total = jnp.zeros_like(x)
    for index, w_ref in enumerate(w_refs):
        total = total + dot_nt(joined_ref[place_ref[index]], w_ref[...])
    scale = lax.rsqrt(jnp.mean(x * x, axis=1, keepdims=True) + norm_eps)
    lifted = total * gain_ref[...]
    inner = jnp.mean(lifted * x, axis=1, keepdims=True)
    out_ref[...] = grad_mixed_ref[...] + scale * lifted - x * (scale * scale * scale * inner)


def expert_kernel(sides, steps, base_ref, bits_ref, *refs):
    token_refs, refs = refs[: 2 * sides], refs[2 * sides :]
    w_in_ref, w_out_ref, refs = refs[0], refs[1], refs[2:]
    out_refs, refs = refs[:sides], refs[sides:]
    back_refs, refs = (refs[:1], *(refs[i : i + 2] for i in range(1, 2 * sides - 1, 2))), refs[2 * sides - 1 :]
    send_refs, keep_refs, refs = refs[:steps], refs[steps : 2 * steps], refs[2 * steps :]
    x_scr, g_scr, gate_scr, rank_scr, out_acc, back_acc, gg_acc, sum_acc = refs
    group, step = pl.program_id(0), pl.program_id(1)
    chosen = base_ref[0] + step
    tokens = token_refs[0].shape[1] - TAIL

    @pl.when(step == 0)
    def _():
        out_acc[...] = jnp.zeros_like(out_acc)
        back_acc[...] = jnp.zeros_like(back_acc)
        gg_acc[...] = jnp.zeros_like(gg_acc)

    blocks = EXPERTS // 8

    def matches(s):
        return iota((MOST, tokens), 0) == rank_scr[s : s + 1].astype(jnp.int32)

    def bring(rows_ref, grads_ref):
        for s in range(GROUP):
            wide = rows_ref[s, tokens:].astype(f32)
            wide = wide[:8] + wide[8:]
            ranks = grads_ref[s, tokens:].astype(f32)[:8]
            gate_row = jnp.zeros((1, tokens), f32)
            rank_row = jnp.zeros((1, tokens), f32)
            for b in range(blocks):
                lanes = slice(b * tokens, (b + 1) * tokens)
                mine = iota((8, tokens), 0) + 8 * b == chosen
                gate_row += jnp.sum(jnp.where(mine, wide[:, lanes], 0.0), axis=0, keepdims=True)
                rank_row += jnp.sum(jnp.where(mine, ranks[:, lanes], 0.0), axis=0, keepdims=True)
            rank_scr[s : s + 1] = rank_row
            hit = iota((MOST, tokens), 0) == rank_row.astype(jnp.int32)
            spot = jnp.where(hit, 1.0, 0.0).astype(bf16)
            at = slice(s * MOST, (s + 1) * MOST)
            x_scr[at] = dot(spot, rows_ref[s, :tokens]).astype(bf16)
            g_scr[at] = dot(spot, grads_ref[s, :tokens]).astype(bf16)
            gate_scr[at] = jnp.sum(jnp.where(hit, gate_row, 0.0), axis=1, keepdims=True)

    if sides == 1:
        bring(*token_refs)
    else:
        for side in range(sides):
            pl.when(group == side)(functools.partial(bring, *token_refs[2 * side : 2 * side + 2]))

    x, g, gate = x_scr[...], g_scr[...], gate_scr[...]
    act = dot(x, w_in_ref[0])
    gate_part, up_part = act[:, :FF], act[:, FF:]
    sig = jax.nn.sigmoid(gate_part)
    silu = gate_part * sig
    hidden = silu * up_part
    raw = dot_nt(g, w_out_ref[0])
    grad_gates = jnp.sum(hidden * raw, axis=1, keepdims=True)
    scaled = (hidden * gate).astype(bf16)
    produced = dot(scaled, w_out_ref[0]).astype(bf16)
    grad_hidden = raw * gate
    grad_act = jnp.concatenate(
        [grad_hidden * up_part * sig * (1.0 + gate_part * (1.0 - sig)), grad_hidden * silu], axis=1
    ).astype(bf16)
    grad_rows = dot_nt(grad_act, w_in_ref[0]).astype(bf16)

    tall, low = x.shape[1] // 2, FF // 2
    half = tall + low

    @pl.when(group == 0)
    def _():
        sum_acc[step] = jnp.zeros(sum_acc.shape[1:], f32)

    for h in range(2):
        sum_acc[step, h * half : h * half + tall] += dot_tn(
            x_scr[:, h * tall : (h + 1) * tall], grad_act
        )
        sum_acc[step, h * half + tall : (h + 1) * half] += dot_tn(
            scaled[:, h * low : (h + 1) * low], g_scr[...]
        )

    for index in range(steps):

        @pl.when((group == pl.num_programs(0) - 1) & (step == index))
        def _():
            bit = bits_ref[index]
            other = pl.ds(pl.multiple_of((1 - bit) * half, half), half)
            send_refs[index][...] = sum_acc[index, other].astype(bf16)
            own = pl.ds(pl.multiple_of(bit * half, half), half)
            keep_refs[index][...] = sum_acc[index, own].astype(bf16)

    for s in range(GROUP):
        hit = matches(s)
        spot = jnp.where(hit, 1.0, 0.0).astype(bf16)
        at = slice(s * MOST, (s + 1) * MOST)
        out_acc[s] += dot_tn(spot, produced[at])
        back_acc[s] += dot_tn(spot, grad_rows[at])
        row = jnp.sum(jnp.where(hit, grad_gates[at], 0.0), axis=0, keepdims=True)
        wide = jnp.concatenate([jnp.broadcast_to(row, (8, tokens))] * blocks, axis=1)
        index = iota(wide.shape, 1) // tokens * 8 + iota(wide.shape, 0)
        gg_acc[s] += jnp.where(index == chosen, wide, 0.0)

    for side in range(sides):
        ours = True if sides == 1 else group == side

        @pl.when((step == steps - 1) & ours)
        def _():
            for s in range(GROUP):
                out_refs[side][s] = out_acc[s].astype(bf16)
                each = GROUP // len(back_refs[side])
                back_ref, at = back_refs[side][s // each], s % each
                back_ref[at, :tokens] = back_acc[s].astype(bf16)
                high, low_part = split_bits(gg_acc[s])
                back_ref[at, tokens:] = jnp.concatenate(
                    [high.astype(f32), low_part.astype(f32)], axis=0
                ).astype(bf16)


def run_experts(base, begin, bits, sides, w_in, w_out, steps):
    sources, full, width = sides[0][0].shape
    tokens = full - TAIL
    count = len(sides)
    groups = count if count > 1 else sources // GROUP
    half = (width + FF) // 2
    by_group = (lambda g, e, *_: (0, 0, 0)) if count > 1 else (lambda g, e, *_: (g, 0, 0))
    by_expert = lambda g, e, base, bits, begin: (begin[0] + e, 0, 0)

    def kernel(base_ref, bits_ref, begin_ref, *refs):
        expert_kernel(count, steps, base_ref, bits_ref, *refs)

    single = pl.Buffered(1)
    tokens_mode = single if count > 1 else None
    half_spec = pl.BlockSpec((half, width), lambda g, e, *_: (0, 0), pipeline_mode=single)
    results = pl.pallas_call(
        kernel,
        grid_spec=pltpu.PrefetchScalarGridSpec(
            num_scalar_prefetch=3,
            grid=(groups, steps),
            in_specs=[
                *[pl.BlockSpec((GROUP, full, width), by_group, pipeline_mode=tokens_mode)]
                * (2 * count),
                pl.BlockSpec((1, width, 2 * FF), by_expert),
                pl.BlockSpec((1, FF, width), by_expert),
            ],
            out_specs=[
                *[pl.BlockSpec((GROUP, tokens, width), by_group, pipeline_mode=single)] * count,
                pl.BlockSpec((GROUP, full, width), by_group, pipeline_mode=single),
                *[pl.BlockSpec((GROUP // 2, full, width), by_group, pipeline_mode=single)]
                * (2 * count - 2),
                *[half_spec] * (2 * steps),
            ],
            scratch_shapes=[
                pltpu.VMEM((GROUP * MOST, width), bf16),
                pltpu.VMEM((GROUP * MOST, width), bf16),
                pltpu.VMEM((GROUP * MOST, 1), f32),
                pltpu.VMEM((8, tokens), f32),
                pltpu.VMEM((GROUP, tokens, width), f32),
                pltpu.VMEM((GROUP, tokens, width), f32),
                pltpu.VMEM((GROUP, 8, width), f32),
                pltpu.VMEM((steps, 2 * half, width), f32),
            ],
        ),
        out_shape=[
            *[jax.ShapeDtypeStruct((sources, tokens, width), bf16)] * count,
            jax.ShapeDtypeStruct((sources, full, width), bf16),
            *[jax.ShapeDtypeStruct((GROUP // 2, full, width), bf16)] * (2 * count - 2),
            *[jax.ShapeDtypeStruct((half, width), bf16)] * (2 * steps),
        ],
        compiler_params=params(62),
        cost_estimate=hint(11 * steps * groups),
        name="experts",
    )(base.reshape(1), bits, begin.reshape(1), *[v for side in sides for v in side], w_in, w_out)
    outs, results = results[:count], results[count:]
    backs, results = results[: 2 * count - 1], results[2 * count - 1 :]
    return outs, backs, results[:steps], results[steps:]


def sum_backs_kernel(*refs):
    own, rest, out_ref = refs[:2], refs[2:6], refs[6]
    total = own[0][...].astype(f32) + own[1][...].astype(f32)
    early = rest[0][...].astype(f32) + rest[2][...].astype(f32)
    late = rest[1][...].astype(f32) + rest[3][...].astype(f32)
    out_ref[...] = (total + jnp.where(pl.program_id(0) < GROUP // 2, early, late)).astype(bf16)


def sum_backs(own, came):
    _, full, width = own[0].shape
    spec = lambda index: pl.BlockSpec((1, full, width), lambda i: (index(i), 0, 0))
    first = spec(lambda i: jnp.minimum(i, GROUP // 2 - 1))
    second = spec(lambda i: jnp.maximum(i - GROUP // 2, 0))
    return pl.pallas_call(
        sum_backs_kernel,
        grid=(GROUP,),
        in_specs=[spec(lambda i: i)] * 2 + [first, second] * 2,
        out_specs=spec(lambda i: i),
        out_shape=jax.ShapeDtypeStruct((GROUP, full, width), bf16),
        compiler_params=params(32),
        name="sum_backs",
    )(*own, *came)


def trade(value, axis, bit):
    size = lax.axis_size(axis)
    return lax.ppermute(value, axis, [(i, i ^ bit) for i in range(size)])


def pick(value, index):
    return lax.dynamic_index_in_dim(value, index, axis=0, keepdims=False)


def after(value, *others):
    return lax.optimization_barrier((value, *others))[0]


def add_split_kernel(bit_ref, keep_other, came_other, keep_own, came_own, send_ref, own_ref):
    send_ref[...] = (keep_other[...].astype(f32) + came_other[...].astype(f32)).astype(bf16)
    own_ref[...] = (keep_own[...].astype(f32) + came_own[...].astype(f32)).astype(bf16)


def add_split(bit, keep, came):
    rows, width = came.shape
    tile = 128
    tiles = rows // 2 // tile
    other = pl.BlockSpec((tile, width), lambda i, bit: ((1 - bit[0]) * tiles + i, 0))
    own = pl.BlockSpec((tile, width), lambda i, bit: (bit[0] * tiles + i, 0))
    result = pl.BlockSpec((tile, width), lambda i, bit: (i, 0))
    return pl.pallas_call(
        add_split_kernel,
        grid_spec=pltpu.PrefetchScalarGridSpec(
            num_scalar_prefetch=1,
            grid=(tiles,),
            in_specs=[other, other, own, own],
            out_specs=[result, result],
        ),
        out_shape=[jax.ShapeDtypeStruct((rows // 2, width), bf16)] * 2,
        cost_estimate=hint(60),
        name="add_split",
    )(bit.reshape(1), keep, came, keep, came)


def add_pairs_kernel(a_ref, b_ref, c_ref, d_ref, *refs):
    out_ref = refs[-1]
    out_ref[0, 0] = (a_ref[...].astype(f32) + b_ref[...].astype(f32)).astype(bf16)
    out_ref[1, 0] = (c_ref[...].astype(f32) + d_ref[...].astype(f32)).astype(bf16)


def add_pairs(a, b, c, d, before):
    rows, width = a.shape
    tile = 128
    chunk = 0 if before is None else 1
    kept = () if before is None else (before,)
    return pl.pallas_call(
        add_pairs_kernel,
        grid=(rows // tile,),
        in_specs=[pl.BlockSpec((tile, width), lambda i: (i, 0))] * 4
        + [pl.BlockSpec(memory_space=pl.ANY)] * len(kept),
        out_specs=pl.BlockSpec((2, 1, tile, width), lambda i: (0, chunk, i, 0)),
        out_shape=jax.ShapeDtypeStruct((2, 2, rows, width), bf16),
        input_output_aliases={} if before is None else {4: 0},
        cost_estimate=hint(60),
        name="add_pairs",
    )(a, b, c, d, *kept)


def put_kernel(count, spots, *refs):
    pieces, refs = refs[:count], refs[-4:]
    gin_ref, gout_ref, buffer, sems = refs
    step, steps = pl.program_id(0), pl.num_programs(0)
    rows = buffer.shape[2]
    rest = FF - rows

    def each(at, index, slot, act):
        first = 3 * (index * steps + at)
        expert, half, quarter = spots[first], spots[first + 1], spots[first + 2]
        top = pl.multiple_of(half * FF, FF)

        @pl.when(quarter == 0)
        def _():
            act(
                pltpu.make_async_copy(
                    buffer.at[slot, index], gin_ref.at[expert, pl.ds(top, rows)], sems.at[slot, index, 0]
                )
            )

        @pl.when(quarter == 1)
        def _():
            act(
                pltpu.make_async_copy(
                    buffer.at[slot, index, pl.ds(0, rest)],
                    gin_ref.at[expert, pl.ds(pl.multiple_of(top + rows, rest), rest)],
                    sems.at[slot, index, 0],
                )
            )
            act(
                pltpu.make_async_copy(
                    buffer.at[slot, index, pl.ds(rest, rows - rest)],
                    gout_ref.at[expert, pl.ds(pl.multiple_of(half * (FF // 2), FF // 2), FF // 2)],
                    sems.at[slot, index, 1],
                )
            )

    slot = step % 2
    for index in range(count):

        @pl.when(step >= 2)
        def _():
            each(step - 2, index, slot, lambda copy: copy.wait())

        buffer[slot, index] = pieces[index][0, 0].astype(f32)
        each(step, index, slot, lambda copy: copy.start())

    @pl.when(step == steps - 1)
    def _():
        for index in range(count):
            each(steps - 2, index, 1 - slot, lambda copy: copy.wait())
            each(steps - 1, index, slot, lambda copy: copy.wait())


def put(spots, pieces, experts, before):
    paths, chunks, rows, width = pieces[0].shape
    kept = () if before is None else tuple(before)
    count, steps = len(pieces), paths * chunks
    anywhere = pl.BlockSpec(memory_space=pl.ANY)
    return pl.pallas_call(
        functools.partial(put_kernel, count),
        grid_spec=pltpu.PrefetchScalarGridSpec(
            num_scalar_prefetch=1,
            grid=(steps,),
            in_specs=[
                pl.BlockSpec((1, 1, rows, width), lambda i, c: (i // chunks, i % chunks, 0, 0))
            ]
            * count
            + [anywhere] * len(kept),
            out_specs=[anywhere] * 2,
            scratch_shapes=[
                pltpu.VMEM((2, count, rows, width), f32),
                pltpu.SemaphoreType.DMA((2, count, 2)),
            ],
        ),
        out_shape=[
            jax.ShapeDtypeStruct((experts, width, 2 * FF), f32),
            jax.ShapeDtypeStruct((experts, FF, width), f32),
        ],
        input_output_aliases={} if before is None else {1 + count: 0, 2 + count: 1},
        compiler_params=params(40),
        cost_estimate=hint(1),
        name="put",
    )(spots, *pieces, *kept)


def plane_parts(value, *between):
    half = value.shape[0] // 2
    along, across = trade(value, "row", 1), trade(value, "row", 2)
    there = trade(value, "col", 1)
    along, across = after((along, across), *between)
    far = jnp.concatenate(
        [trade(along[:half], "row", 2), trade(across[half:], "row", 1)], axis=0
    )
    return [value, along, across, far, there] + [
        trade(part, "col", 1) for part in (along, across, far)
    ]


def body(
    block_input,
    seq_lengths,
    routes,
    norm1_gain,
    w_qkv,
    w_heads,
    norm2_gain,
    router,
    w_expert_in,
    w_expert_out,
    out_grad,
):
    tok_rows, batches, width = block_input.shape
    dp_size = lax.axis_size("dp")
    plane = lax.axis_size("row") * lax.axis_size("col")
    packed = tok_rows * plane
    tokens = tok_rows * batches
    dp_at = lax.axis_index("dp").astype(jnp.int32)
    sds = jax.ShapeDtypeStruct

    x = jnp.transpose(block_input, (1, 0, 2)).reshape(tokens, width)
    og = jnp.transpose(out_grad, (1, 0, 2)).reshape(tokens, width)
    scale1 = lax.rsqrt(jnp.mean(x * x, axis=1, keepdims=True) + norm_eps)
    normed1 = (x * scale1 * norm1_gain).astype(bf16)
    flat_routes = jnp.transpose(routes, (1, 0, 2)).reshape(tokens, -1)
    used = jnp.any(
        flat_routes[None] == jnp.arange(EXPERTS, dtype=jnp.int32)[:, None, None], axis=2
    )
    before = (
        jnp.arange(tokens, dtype=jnp.int32)[:, None] < jnp.arange(tokens, dtype=jnp.int32)[None, :]
    )
    counted = jnp.dot(used.astype(bf16), before.astype(bf16), preferred_element_type=f32)
    rank = jnp.where(used, counted, -1.0).astype(bf16)
    rank_rows = jnp.transpose(rank.reshape(EXPERTS // 8, 8, tokens), (1, 0, 2)).reshape(8, -1)
    grads_in = lax.all_gather(
        jnp.concatenate([og.astype(bf16), rank_rows, jnp.zeros_like(rank_rows)], axis=0),
        "dp",
        axis=0,
        tiled=False,
    )

    segment, position = pack_tables(seq_lengths[0], packed)
    inverse = jnp.exp(
        -(2.0 * jnp.arange(HEAD_SIZE // 2, dtype=f32) / HEAD_SIZE) * math.log(rope_base)
    )
    angles = position.astype(f32)[:, :, None] * inverse[None, None, :]
    cosine, sine = jnp.cos(angles), jnp.sin(angles)
    cosine = jnp.concatenate([cosine] * 4, axis=2)
    sine = jnp.concatenate([-sine, sine, -sine, sine], axis=2)
    seg_rows, seg_cols = segment[:, :, None], segment[:, None, :]

    row = lax.axis_index("row").astype(jnp.int32)
    col = lax.axis_index("col").astype(jnp.int32)
    places = jnp.stack([(row ^ k) * 2 + (col ^ c) for c in range(2) for k in range(4)])
    w_group = lax.all_to_all(w_qkv, "col", split_axis=1, concat_axis=0, tiled=True)
    parts = plane_parts(
        normed1.reshape(batches, tok_rows, width), cosine, sine, seg_rows, seg_cols, w_group
    )

    per_m = lambda m, *_: (m, 0, 0)
    const = lambda m, *_: (0, 0)
    by_device = lambda m, *_: (0, m, 0, 0)
    table_specs = [
        pl.BlockSpec((1, packed, 128), per_m),
        pl.BlockSpec((1, packed, 128), per_m),
        pl.BlockSpec((1, packed, 1), per_m),
        pl.BlockSpec((1, 1, packed), per_m),
    ]
    x_all, qkv, head_out, lse = pl.pallas_call(
        attn_fwd_kernel,
        grid_spec=pltpu.PrefetchScalarGridSpec(
            num_scalar_prefetch=1,
            grid=(batches,),
            in_specs=[
                *[pl.BlockSpec((1, tok_rows, width), per_m)] * 8,
                pl.BlockSpec((width, 256), const),
                *table_specs,
            ],
            out_specs=[
                pl.BlockSpec((1, packed, width), per_m),
                pl.BlockSpec((1, packed, 256), per_m),
                pl.BlockSpec((plane, 1, tok_rows, 128), by_device),
                pl.BlockSpec((1, packed, 128), per_m),
            ],
            scratch_shapes=[pltpu.VMEM((packed, 256), f32)],
        ),
        out_shape=[
            sds((batches, packed, width), bf16),
            sds((batches, packed, 256), bf16),
            sds((plane, batches, tok_rows, 128), bf16),
            sds((batches, packed, 128), f32),
        ],
        compiler_params=params(48),
        cost_estimate=hint(13),
        name="attn_fwd",
    )(places, *parts, w_group, cosine, sine, seg_rows, seg_cols)

    heads = lax.all_to_all(
        head_out.reshape(plane, tokens, 128), PLANE, split_axis=0, concat_axis=0, tiled=True
    )
    gain1, gain2 = norm1_gain.reshape(1, width), norm2_gain.reshape(1, width)
    router_t = jnp.transpose(router)
    w_heads_parts = plane_parts(after(w_heads, parts[3]), head_out)

    def with_places(kernel, count, outs, mib, name):
        in_vmem = pl.BlockSpec(memory_space=pltpu.VMEM)
        return pl.pallas_call(
            kernel,
            in_specs=[pl.BlockSpec(memory_space=pltpu.SMEM)] + [in_vmem] * count,
            out_shape=outs,
            compiler_params=params(mib),
            name=name,
        )

    mixed, send, gates = with_places(
        token_fwd_kernel,
        13,
        [
            sds((tokens, width), f32),
            sds((tokens + TAIL, width), bf16),
            sds((EXPERTS, tokens), f32),
        ],
        32,
        "token_fwd",
    )(places, *w_heads_parts, heads, x, gain2, router_t, rank)

    rows_in = lax.all_gather(send, "dp", axis=0, tiled=False)
    w_group_parts = plane_parts(after(w_group, send))
    here = w_expert_in.shape[0]
    first, second = row % 2, (row // 2) % 2
    bits = jnp.stack([first, second])
    shared = here == 8
    chunks = []
    if shared:
        grads_there = trade(grads_in, "col", 1)
        rows_in = after(rows_in, w_group_parts, grads_there)
        rows_there = trade(rows_in, "col", 1)
        own_backs, came_backs, outs = [], [], []
        for index in range(2):
            begin = 4 * col + 2 * index
            out, back, away, kept = run_experts(
                dp_at * here + begin,
                begin,
                bits,
                ((rows_in, grads_in), (rows_there, grads_there)),
                w_expert_in,
                w_expert_out,
                2,
            )
            own_backs.append(back[0])
            came_backs += [trade(value, "col", 1) for value in back[1:]]
            outs += [out[0], trade(out[1], "col", 1)]
            chunks.append((away, kept))
            rows_there = after(rows_there, back[0])
            last = back[0]
    else:
        zero = jnp.zeros_like(dp_at)
        outs, (back,), away, kept = run_experts(
            dp_at * here,
            zero,
            jnp.zeros_like(bits),
            ((rows_in, grads_in),),
            w_expert_in,
            w_expert_out,
            1,
        )

    flips = (1, 2)
    halves = []

    def first_sum(away, kept, *order):
        kept = after(kept, *order)
        came = [trade(away[path], "row", flips[path]) for path in range(2)]
        return [add_split(bits[1 - path], kept[path], came[path]) for path in range(2)]

    def second_sum(halves, before, *order):
        came = [trade(halves[path][0], "row", flips[1 - path]) for path in range(2)]
        own = after((halves[0][1], halves[1][1]), *order)
        return add_pairs(own[0], came[0], own[1], came[1], before)

    if shared:
        halves.append(first_sum(*chunks[0], last))
        own_backs = after(own_backs, halves[0])
        back = sum_backs(own_backs, came_backs)
        halves.append(first_sum(*chunks[1], back))
        ready_a = second_sum(halves[0], None, halves[1])
    back = lax.psum_scatter(
        back.reshape(dp_size * (tokens + TAIL), width), "dp", scatter_dimension=0, tiled=True
    )
    if shared:
        back = after(back, ready_a)
    grad_mixed, grad_heads, sums = with_places(
        token_bwd_kernel,
        16,
        [
            sds((tokens, width), f32),
            sds((plane, tokens, 128), bf16),
            sds((plane, 128 + TAIL, width), bf16),
        ],
        40,
        "token_bwd",
    )(places, *w_heads_parts, back, mixed, og, gates, heads, gain2, router_t, send)
    sums = lax.psum_scatter(
        sums.reshape(plane * (128 + TAIL), width), PLANE, scatter_dimension=0, tiled=True
    )
    grad_heads = lax.all_to_all(grad_heads, PLANE, split_axis=0, concat_axis=0, tiled=True)

    if shared:
        ready_b = second_sum(halves[1], ready_a, grad_heads)
        grad_heads = after(grad_heads, ready_b)

    grad_joined, grad_w_qkv = pl.pallas_call(
        attn_bwd_kernel,
        grid=(batches,),
        in_specs=[
            pl.BlockSpec((1, packed, width), per_m),
            pl.BlockSpec((width, 256), const),
            *table_specs,
            pl.BlockSpec((1, packed, 256), per_m),
            pl.BlockSpec((1, packed, 128), per_m),
            pl.BlockSpec((plane, 1, tok_rows, 128), by_device),
        ],
        out_specs=[
            pl.BlockSpec((plane, 1, tok_rows, 256), by_device),
            pl.BlockSpec((2, width // 2 + TAIL, 256), lambda m: (0, 0, 0)),
        ],
        out_shape=[
            sds((plane, batches, tok_rows, 256), bf16),
            sds((2, width // 2 + TAIL, 256), bf16),
        ],
        scratch_shapes=[
            pltpu.VMEM((width, 256), f32),
            pltpu.VMEM((packed, 128), f32),
            pltpu.VMEM((packed, 128), f32),
        ],
        compiler_params=params(48),
        cost_estimate=hint(18),
        name="attn_bwd",
    )(
        x_all, w_group, cosine, sine, seg_rows, seg_cols, qkv, lse,
        grad_heads.reshape(plane, batches, tok_rows, 128),
    )

    if shared:
        along, across = trade(ready_b, "row", 1), trade(ready_b, "row", 2)
    grad_joined = lax.all_to_all(
        grad_joined.reshape(plane, tokens, 256), PLANE, split_axis=0, concat_axis=0, tiled=True
    )
    grad_w_qkv = lax.all_to_all(grad_w_qkv, "col", split_axis=0, concat_axis=0, tiled=True)
    produced = sum(value.astype(f32) for value in outs).astype(bf16)
    sums, produced = lax.optimization_barrier((sums, produced))
    sums, grad_w_qkv = lax.psum((sums, grad_w_qkv), "dp")
    produced = lax.psum_scatter(
        produced.reshape(dp_size * tokens, width), "dp", scatter_dimension=0, tiled=True
    )
    block_output = mixed + produced.astype(f32)
    if shared:
        along, across = after((along, across), grad_joined)
        fars = (trade(across[:1], "row", 1), trade(along[1:], "row", 2))
    input_grad = with_places(token_end_kernel, 12, sds((tokens, width), f32), 32, "token_end")(
        places, *w_group_parts, grad_joined, x, gain1, grad_mixed
    )

    if shared:
        fronts = (ready_b, along, across)
        fronts_there = tuple(trade(value, "col", 1) for value in fronts)

        def spots(owner, path, chunk, k):
            pair = (first ^ (k & 1), second ^ (k >> 1))
            return [4 * owner + 2 * chunk + path, pair[path], pair[1 - path]]

        def front_spots(owner):
            return jnp.stack(
                [v for k in range(3) for p in range(2) for c in range(2) for v in spots(owner, p, c, k)]
            )

        def far_spots(owner):
            return jnp.stack([v for p in range(2) for c in range(2) for v in spots(owner, p, c, 3)])

        first_put = put(front_spots(col), fronts, here, None)
        grad_experts = put(front_spots(1 - col), fronts_there, here, first_put)
        sums, grad_w_qkv = after((sums, grad_w_qkv), grad_experts)

    sums = sums.astype(f32)
    heads_grad = sums[:128]
    half = width // 2
    qkv_sums = grad_w_qkv.astype(f32)
    grad_w_qkv = jnp.concatenate([qkv_sums[0, :half], qkv_sums[1, :half]], axis=1)
    scaled = qkv_sums[:, half : half + 4] + qkv_sums[:, half + 4 : half + 8]
    scaled = jnp.sum(scaled, axis=0).reshape(1, width)
    rest = plane_parts(
        jnp.concatenate([scaled, sums[128:], jnp.zeros((15, width), f32)], axis=0)
    )
    per = EXPERTS // plane
    norm1_grad = sum(part[0] for part in rest[:4]) / norm1_gain
    norm2_grad = sum(part[1 + per] for part in rest)
    router_grad = sum(
        jnp.where(
            places[index] == jnp.arange(plane, dtype=jnp.int32)[:, None, None],
            part[None, 1 : 1 + per],
            0.0,
        )
        for index, part in enumerate(rest)
    )
    router_grad = jnp.transpose(router_grad.reshape(EXPERTS, width))

    if shared:
        fars = after(fars, grad_experts)
        fars_there = tuple(trade(value, "col", 1) for value in fars)
        grad_experts = put(far_spots(col), fars, here, grad_experts)
        grad_experts = after(grad_experts, block_output, heads_grad, grad_w_qkv, input_grad)
        grad_experts = put(far_spots(1 - col), fars_there, here, grad_experts)
        grad_w_in, grad_w_out = grad_experts
    else:
        total = lax.psum(jnp.stack([kept[0], away[0]]), PLANE).astype(f32)
        total = total.reshape(here, 2, (width + FF) // 2, width)
        grad_w_in = total[:, :, : width // 2].reshape(here, width, 2 * FF)
        grad_w_out = total[:, :, width // 2 :].reshape(here, FF, width)

    def placed(value):
        return jnp.transpose(value.reshape(batches, tok_rows, width), (1, 0, 2))

    return (
        placed(block_output),
        placed(input_grad),
        norm1_grad,
        grad_w_qkv,
        heads_grad,
        norm2_grad,
        router_grad,
        grad_w_in,
        grad_w_out,
    )


def solution(mesh):
    return jax.shard_map(
        body,
        mesh=mesh,
        in_specs=(
            P(("dp", "row", "col"), None, None),
            P("dp", None, None),
            P(("dp", "row", "col"), None, None),
            P(),
            P("col", "row"),
            P(("row", "col"), None),
            P(),
            P(),
            P("dp", None, None),
            P("dp", None, None),
            P(("dp", "row", "col"), None, None),
        ),
        out_specs=(
            P(("dp", "row", "col"), None, None),
            P(("dp", "row", "col"), None, None),
            P(),
            P("col", "row"),
            P(("row", "col"), None),
            P(),
            P(),
            P("dp", None, None),
            P("dp", None, None),
        ),
        check_vma=False,
    )
```

```python
import functools
import math

import jax
import jax.numpy as jnp
from jax import lax
from jax.experimental import pallas as pl
from jax.experimental.pallas import tpu as pltpu
from jax.sharding import PartitionSpec as P

HEAD_SIZE = 64
EXPERTS = 32
FF = 512
WIDTH = 1024
GROUP = 4
MOST = 128
TAIL = 16

norm_eps = 1e-06
rope_base = 10000.0
neg_large = -1e30
inv_root = HEAD_SIZE ** (-0.5)

f32 = jnp.float32
bf16 = jnp.bfloat16
PLANE = ("row", "col")


def dot(a, b):
    return lax.dot_general(a, b, (((1,), (0,)), ((), ())), preferred_element_type=f32)


def dot_nt(a, b):
    return lax.dot_general(a, b, (((1,), (1,)), ((), ())), preferred_element_type=f32)


def dot_tn(a, b):
    return lax.dot_general(a, b, (((0,), (0,)), ((), ())), preferred_element_type=f32)


def split_bits(value):
    high = value.astype(bf16)
    return high, (value - high.astype(f32)).astype(bf16)


def iota(shape, dim):
    return lax.broadcasted_iota(jnp.int32, shape, dim)


def params(mib, **more):
    return pltpu.CompilerParams(vmem_limit_bytes=mib * 1024 * 1024, **more)


def hint(micros):
    return pl.CostEstimate(flops=1_000_000_000 * micros, bytes_accessed=0, transcendentals=0)


def pack_tables(lengths, packed_length):
    seq_ends = jnp.cumsum(lengths, axis=1)
    starts = seq_ends - lengths
    places = jnp.arange(packed_length, dtype=jnp.int32)
    segment = jnp.sum((places[None, :, None] >= seq_ends[:, None, :]).astype(jnp.int32), axis=2)
    labels = jnp.arange(lengths.shape[1], dtype=jnp.int32)
    seq_start = jnp.sum(
        jnp.where(segment[:, :, None] == labels[None, None, :], starts[:, None, :], 0), axis=2
    )
    return (segment, places[None, :] - seq_start)


def swap_halves(value):
    lane = iota(value.shape, 1) % HEAD_SIZE
    width = value.shape[1]
    return jnp.where(
        lane < HEAD_SIZE // 2,
        pltpu.roll(value, width - HEAD_SIZE // 2, 1),
        pltpu.roll(value, HEAD_SIZE // 2, 1),
    )


def fold(value):
    return value + pltpu.roll(value, HEAD_SIZE, 1)


def twice(pair):
    rolled = pltpu.roll(pair, HEAD_SIZE, 1)
    first = iota(pair.shape, 1) < HEAD_SIZE
    return jnp.where(first, pair, rolled).astype(bf16), jnp.where(first, rolled, pair).astype(bf16)


def block_mask(seg_rows, seg_cols, offset, size, limit):
    same = seg_rows[offset : offset + size] == seg_cols[:, :limit]
    rows = iota((size, limit), 0) + offset
    return same & (rows >= iota((size, limit), 1))


Q_BLOCK = 256


def attn_fwd_kernel(place_ref, *refs):
    part_refs, refs = refs[:8], refs[8:]
    w_ref, cos_ref, sin_ref, segr_ref, segc_ref, x_ref, qkv_ref, out_ref, lse_ref, joined_ref = refs
    rows = part_refs[0].shape[1]
    packed = 8 * rows
    for index, part_ref in enumerate(part_refs):
        at = pl.ds(pl.multiple_of(place_ref[index] * rows, rows), rows)
        part = part_ref[0]
        x_ref[0, at] = part
        joined_ref[at] = dot(part, w_ref[...])
    joined = joined_ref[...]
    cosine, sine = cos_ref[0], sin_ref[0]
    first = iota((packed, 128), 1) < HEAD_SIZE
    query = joined[:, :128]
    pair = joined[:, 128:]
    query = query * cosine + swap_halves(query) * sine
    pair = jnp.where(first, pair * cosine + swap_halves(pair) * sine, pair)
    query = query.astype(bf16)
    pair16 = pair.astype(bf16)
    qkv_ref[0, :, :128] = query
    qkv_ref[0, :, 128:] = pair16
    keys, values = twice(pair16.astype(f32))
    seg_rows, seg_cols = segr_ref[0], segc_ref[0]
    lane = iota((Q_BLOCK, 128), 1)
    for offset in range(0, packed, Q_BLOCK):
        limit = offset + Q_BLOCK
        mask = block_mask(seg_rows, seg_cols, offset, Q_BLOCK, limit)
        outs, sums = [], []
        for head in range(2):
            mine = (lane < HEAD_SIZE) if head == 0 else (lane >= HEAD_SIZE)
            rows_q = jnp.where(mine, query[offset:limit], jnp.zeros((), bf16))
            scores = dot_nt(rows_q, keys[:limit]) * inv_root
            scores = jnp.where(mask, scores, neg_large)
            top = jnp.max(scores, axis=1, keepdims=True)
            part = jnp.exp(scores - top)
            total = jnp.sum(part, axis=1, keepdims=True)
            weights = (part * (1.0 / total)).astype(bf16)
            outs.append(dot(weights, values[:limit]))
            sums.append(top + jnp.log(total))
        merged = jnp.where(lane < HEAD_SIZE, outs[0], outs[1]).astype(bf16)
        out_ref[offset // rows : limit // rows, 0] = merged.reshape(Q_BLOCK // rows, rows, 128)
        lse_ref[0, offset:limit] = jnp.where(lane < HEAD_SIZE, sums[0], sums[1])


def attn_bwd_kernel(
    x_ref, w_ref, cos_ref, sin_ref, segr_ref, segc_ref, qkv_ref, lse_ref, grad_ref,
    joined_ref, weight_ref, total_ref, dk_ref, dv_ref,
):
    devices, _, rows, _ = grad_ref.shape
    packed = devices * rows
    m = pl.program_id(0)
    query = qkv_ref[0, :, :128]
    keys, values = twice(qkv_ref[0, :, 128:].astype(f32))
    seg_rows, seg_cols = segr_ref[0], segc_ref[0]
    grad = grad_ref[:, 0].reshape(packed, 128)
    lane = iota((Q_BLOCK, 128), 1)
    zero = jnp.zeros((), bf16)
    dk_ref[...] = jnp.zeros_like(dk_ref)
    dv_ref[...] = jnp.zeros_like(dv_ref)
    grad_query = []
    for offset in range(0, packed, Q_BLOCK):
        limit = offset + Q_BLOCK
        mask = block_mask(seg_rows, seg_cols, offset, Q_BLOCK, limit)
        parts = []
        for head in range(2):
            mine = (lane < HEAD_SIZE) if head == 0 else (lane >= HEAD_SIZE)
            rows_q = jnp.where(mine, query[offset:limit], zero)
            rows_g = jnp.where(mine, grad[offset:limit], zero)
            scores = dot_nt(rows_q, keys[:limit]) * inv_root
            at = head * HEAD_SIZE
            probs = jnp.exp(jnp.where(mask, scores, neg_large) - lse_ref[0, offset:limit, at : at + 1])
            grad_probs = dot_nt(rows_g, values[:limit])
            weighed = probs * grad_probs
            delta = jnp.sum(weighed, axis=1, keepdims=True)
            grad_scores = (weighed - probs * delta).astype(bf16)
            parts.append(dot(grad_scores, keys[:limit]))
            dk_ref[:limit] += dot_tn(grad_scores, rows_q)
            dv_ref[:limit] += dot_tn(probs.astype(bf16), rows_g)
        grad_query.append(jnp.where(lane < HEAD_SIZE, parts[0], parts[1]))
    dq = jnp.concatenate(grad_query, axis=0) * inv_root
    dk = fold(dk_ref[...]) * inv_root
    dv = fold(dv_ref[...])
    cosine, sine = cos_ref[0], sin_ref[0]
    first = iota((packed, 128), 1) < HEAD_SIZE
    dq = dq * cosine - swap_halves(dq) * sine
    dk = dk * cosine - swap_halves(dk) * sine
    joined = jnp.concatenate([dq, jnp.where(first, dk, dv)], axis=1).astype(bf16)
    joined_ref[:, 0] = joined.reshape(devices, rows, 256)
    part = dot_tn(x_ref[0], joined)

    @pl.when(m == 0)
    def _():
        total_ref[...] = part

    @pl.when(m > 0)
    def _():
        total_ref[...] += part

    @pl.when(m == pl.num_programs(0) - 1)
    def _():
        half = weight_ref.shape[1] - TAIL
        high, low = split_bits(total_ref[...] * w_ref[...].astype(f32))
        ones = jnp.ones((8, high.shape[1]), bf16)
        scaled = (dot_nt(ones, high) + dot_nt(ones, low))[:1]
        scaled = jnp.concatenate([scaled[:, i * 256 : (i + 1) * 256] for i in range(4)], axis=0)
        high, low = split_bits(scaled)
        extra = jnp.concatenate(
            [high.astype(f32), low.astype(f32), jnp.zeros((TAIL - 8, 256), f32)], axis=0
        ).astype(bf16)
        for h in range(2):
            weight_ref[h, :half] = total_ref[h * half : (h + 1) * half].astype(bf16)
            weight_ref[h, half:] = extra


def wide_of_dense(dense):
    return jnp.concatenate([dense[8 * b : 8 * b + 8] for b in range(EXPERTS // 8)], axis=1)


def dense_of_wide(wide):
    part = wide.shape[1] // (EXPERTS // 8)
    return jnp.concatenate(
        [wide[:, b * part : (b + 1) * part] for b in range(EXPERTS // 8)], axis=0
    )


def token_fwd_kernel(place_ref, *refs):
    w_refs, refs = refs[:8], refs[8:]
    heads_ref, x_ref, gain_ref, router_ref, rank_ref, mixed_ref, send_ref, gates_ref = refs
    mixed = x_ref[...]
    for index, w_ref in enumerate(w_refs):
        mixed = mixed + dot(heads_ref[place_ref[index]], w_ref[...])
    mixed_ref[...] = mixed
    scale = lax.rsqrt(jnp.mean(mixed * mixed, axis=1, keepdims=True) + norm_eps)
    normed = (mixed * scale * gain_ref[...]).astype(bf16)
    rows = normed.shape[0]
    send_ref[:rows] = normed
    logits = dot_nt(router_ref[...], normed)
    used = rank_ref[...].astype(f32) >= 0
    logits = jnp.where(used, logits, neg_large)
    part = jnp.where(used, jnp.exp(logits - jnp.max(logits, axis=0, keepdims=True)), 0.0)
    gates = part / jnp.sum(part, axis=0, keepdims=True)
    gates_ref[...] = gates
    high, low = split_bits(wide_of_dense(gates))
    send_ref[rows:] = jnp.concatenate([high.astype(f32), low.astype(f32)], axis=0).astype(bf16)


def token_bwd_kernel(place_ref, *refs):
    w_refs, refs = refs[:8], refs[8:]
    (
        back_ref, mixed_ref, out_grad_ref, gates_ref, heads_ref, gain_ref, router_ref, normed_ref,
        grad_mixed_ref, grad_heads_ref, sums_ref,
    ) = refs
    rows = mixed_ref.shape[0]
    tail = back_ref[rows:].astype(f32)
    grad_gates = dense_of_wide(tail[:8] + tail[8:])
    gates = gates_ref[...]
    weighed = gates * grad_gates
    spread = weighed - gates * jnp.sum(weighed, axis=0, keepdims=True)
    high, low = split_bits(spread)
    router = router_ref[...]
    grad_normed = back_ref[:rows].astype(f32) + dot_tn(high, router) + dot_tn(low, router)
    normed = normed_ref[:rows]
    router_grad = dot(high, normed) + dot(low, normed)
    mixed = mixed_ref[...]
    scale = lax.rsqrt(jnp.mean(mixed * mixed, axis=1, keepdims=True) + norm_eps)
    lifted = grad_normed * gain_ref[...]
    gain_grad = jnp.sum(grad_normed * mixed * scale, axis=0, keepdims=True)
    inner = jnp.mean(lifted * mixed, axis=1, keepdims=True)
    grad_mixed = out_grad_ref[...] + scale * lifted - mixed * (scale * scale * scale * inner)
    grad_mixed_ref[...] = grad_mixed
    branch = grad_mixed.astype(bf16)
    for index, w_ref in enumerate(w_refs):
        grad_heads_ref[place_ref[index]] = dot_nt(branch, w_ref[...]).astype(bf16)
    count = heads_ref.shape[0]
    for j in range(count):
        sums_ref[j, :128] = dot_tn(heads_ref[j], branch).astype(bf16)
        part = router_grad[j * (EXPERTS // count) : (j + 1) * (EXPERTS // count)]
        rest = jnp.zeros((TAIL - part.shape[0] - 1, part.shape[1]), f32)
        sums_ref[j, 128:] = jnp.concatenate(
            [part, gain_grad if j == 0 else jnp.zeros_like(gain_grad), rest], axis=0
        ).astype(bf16)


def token_end_kernel(place_ref, *refs):
    w_refs, refs = refs[:8], refs[8:]
    joined_ref, x_ref, gain_ref, grad_mixed_ref, out_ref = refs
    x = x_ref[...]
    total = jnp.zeros_like(x)
    for index, w_ref in enumerate(w_refs):
        total = total + dot_nt(joined_ref[place_ref[index]], w_ref[...])
    scale = lax.rsqrt(jnp.mean(x * x, axis=1, keepdims=True) + norm_eps)
    lifted = total * gain_ref[...]
    inner = jnp.mean(lifted * x, axis=1, keepdims=True)
    out_ref[...] = grad_mixed_ref[...] + scale * lifted - x * (scale * scale * scale * inner)


def expert_kernel(sides, steps, base_ref, bits_ref, *refs):
    token_refs, refs = refs[: 2 * sides], refs[2 * sides :]
    w_in_ref, w_out_ref, refs = refs[0], refs[1], refs[2:]
    out_refs, refs = refs[:sides], refs[sides:]
    back_refs, refs = (refs[:1], *(refs[i : i + 2] for i in range(1, 2 * sides - 1, 2))), refs[2 * sides - 1 :]
    send_refs, keep_refs, refs = refs[:steps], refs[steps : 2 * steps], refs[2 * steps :]
    x_scr, g_scr, gate_scr, rank_scr, out_acc, back_acc, gg_acc, sum_acc = refs
    group, step = pl.program_id(0), pl.program_id(1)
    chosen = base_ref[0] + step
    tokens = token_refs[0].shape[1] - TAIL

    def put_or_add(first, ref, at, value):
        @pl.when(first)
        def _():
            ref[at] = value

        @pl.when(jnp.logical_not(first))
        def _():
            ref[at] += value

    blocks = EXPERTS // 8

    def matches(s):
        return iota((MOST, tokens), 0) == rank_scr[s : s + 1].astype(jnp.int32)

    def bring(rows_ref, grads_ref):
        for s in range(GROUP):
            wide = rows_ref[s, tokens:].astype(f32)
            wide = wide[:8] + wide[8:]
            ranks = grads_ref[s, tokens:].astype(f32)[:8]
            gate_row = jnp.zeros((1, tokens), f32)
            rank_row = jnp.zeros((1, tokens), f32)
            for b in range(blocks):
                lanes = slice(b * tokens, (b + 1) * tokens)
                mine = iota((8, tokens), 0) + 8 * b == chosen
                gate_row += jnp.sum(jnp.where(mine, wide[:, lanes], 0.0), axis=0, keepdims=True)
                rank_row += jnp.sum(jnp.where(mine, ranks[:, lanes], 0.0), axis=0, keepdims=True)
            rank_scr[s : s + 1] = rank_row
            hit = iota((MOST, tokens), 0) == rank_row.astype(jnp.int32)
            spot = jnp.where(hit, 1.0, 0.0).astype(bf16)
            at = slice(s * MOST, (s + 1) * MOST)
            x_scr[at] = dot(spot, rows_ref[s, :tokens]).astype(bf16)
            g_scr[at] = dot(spot, grads_ref[s, :tokens]).astype(bf16)
            gate_scr[at] = jnp.sum(jnp.where(hit, gate_row, 0.0), axis=1, keepdims=True)

    if sides == 1:
        bring(*token_refs)
    else:
        for side in range(sides):
            pl.when(group == side)(functools.partial(bring, *token_refs[2 * side : 2 * side + 2]))

    x, g, gate = x_scr[...], g_scr[...], gate_scr[...]
    act = dot(x, w_in_ref[0])
    gate_part, up_part = act[:, :FF], act[:, FF:]
    sig = jax.nn.sigmoid(gate_part)
    silu = gate_part * sig
    hidden = silu * up_part
    raw = dot_nt(g, w_out_ref[0])
    grad_gates = jnp.sum(hidden * raw, axis=1, keepdims=True)
    scaled = (hidden * gate).astype(bf16)
    produced = dot(scaled, w_out_ref[0]).astype(bf16)
    grad_hidden = raw * gate
    grad_act = jnp.concatenate(
        [grad_hidden * up_part * sig * (1.0 + gate_part * (1.0 - sig)), grad_hidden * silu], axis=1
    ).astype(bf16)
    grad_rows = dot_nt(grad_act, w_in_ref[0]).astype(bf16)

    tall, low = x.shape[1] // 2, FF // 2
    half = tall + low

    for h in range(2):
        part = dot_tn(x_scr[:, h * tall : (h + 1) * tall], grad_act)
        put_or_add(group == 0, sum_acc, (step, slice(h * half, h * half + tall)), part)
        part = dot_tn(scaled[:, h * low : (h + 1) * low], g_scr[...])
        put_or_add(group == 0, sum_acc, (step, slice(h * half + tall, (h + 1) * half)), part)

    for index in range(steps):

        @pl.when((group == pl.num_programs(0) - 1) & (step == index))
        def _():
            bit = bits_ref[index]
            other = pl.ds(pl.multiple_of((1 - bit) * half, half), half)
            send_refs[index][...] = sum_acc[index, other].astype(bf16)
            own = pl.ds(pl.multiple_of(bit * half, half), half)
            keep_refs[index][...] = sum_acc[index, own].astype(bf16)

    for s in range(GROUP):
        hit = matches(s)
        spot = jnp.where(hit, 1.0, 0.0).astype(bf16)
        at = slice(s * MOST, (s + 1) * MOST)
        put_or_add(step == 0, out_acc, s, dot_tn(spot, produced[at]))
        put_or_add(step == 0, back_acc, s, dot_tn(spot, grad_rows[at]))
        row = jnp.sum(jnp.where(hit, grad_gates[at], 0.0), axis=0, keepdims=True)
        wide = jnp.concatenate([jnp.broadcast_to(row, (8, tokens))] * blocks, axis=1)
        index = iota(wide.shape, 1) // tokens * 8 + iota(wide.shape, 0)
        put_or_add(step == 0, gg_acc, s, jnp.where(index == chosen, wide, 0.0))

    for side in range(sides):
        ours = True if sides == 1 else group == side

        @pl.when((step == steps - 1) & ours)
        def _():
            for s in range(GROUP):
                out_refs[side][s] = out_acc[s].astype(bf16)
                each = GROUP // len(back_refs[side])
                back_ref, at = back_refs[side][s // each], s % each
                back_ref[at, :tokens] = back_acc[s].astype(bf16)
                high, low_part = split_bits(gg_acc[s])
                back_ref[at, tokens:] = jnp.concatenate(
                    [high.astype(f32), low_part.astype(f32)], axis=0
                ).astype(bf16)


def run_experts(base, begin, bits, sides, w_in, w_out, steps):
    sources, full, width = sides[0][0].shape
    tokens = full - TAIL
    count = len(sides)
    groups = count if count > 1 else sources // GROUP
    half = (width + FF) // 2
    by_group = (lambda g, e, *_: (0, 0, 0)) if count > 1 else (lambda g, e, *_: (g, 0, 0))
    by_expert = lambda g, e, base, bits, begin: (begin[0] + e, 0, 0)

    def kernel(base_ref, bits_ref, begin_ref, *refs):
        expert_kernel(count, steps, base_ref, bits_ref, *refs)

    single = pl.Buffered(1)
    tokens_mode = single if count > 1 else None
    half_spec = pl.BlockSpec((half, width), lambda g, e, *_: (0, 0), pipeline_mode=single)
    results = pl.pallas_call(
        kernel,
        grid_spec=pltpu.PrefetchScalarGridSpec(
            num_scalar_prefetch=3,
            grid=(groups, steps),
            in_specs=[
                *[pl.BlockSpec((GROUP, full, width), by_group, pipeline_mode=tokens_mode)]
                * (2 * count),
                pl.BlockSpec((1, width, 2 * FF), by_expert),
                pl.BlockSpec((1, FF, width), by_expert),
            ],
            out_specs=[
                *[pl.BlockSpec((GROUP, tokens, width), by_group, pipeline_mode=single)] * count,
                pl.BlockSpec((GROUP, full, width), by_group, pipeline_mode=single),
                *[pl.BlockSpec((GROUP // 2, full, width), by_group, pipeline_mode=single)]
                * (2 * count - 2),
                *[half_spec] * (2 * steps),
            ],
            scratch_shapes=[
                pltpu.VMEM((GROUP * MOST, width), bf16),
                pltpu.VMEM((GROUP * MOST, width), bf16),
                pltpu.VMEM((GROUP * MOST, 1), f32),
                pltpu.VMEM((8, tokens), f32),
                pltpu.VMEM((GROUP, tokens, width), f32),
                pltpu.VMEM((GROUP, tokens, width), f32),
                pltpu.VMEM((GROUP, 8, width), f32),
                pltpu.VMEM((steps, 2 * half, width), f32),
            ],
        ),
        out_shape=[
            *[jax.ShapeDtypeStruct((sources, tokens, width), bf16)] * count,
            jax.ShapeDtypeStruct((sources, full, width), bf16),
            *[jax.ShapeDtypeStruct((GROUP // 2, full, width), bf16)] * (2 * count - 2),
            *[jax.ShapeDtypeStruct((half, width), bf16)] * (2 * steps),
        ],
        compiler_params=params(62),
        cost_estimate=hint(11 * steps * groups),
        name="experts",
    )(base.reshape(1), bits, begin.reshape(1), *[v for side in sides for v in side], w_in, w_out)
    outs, results = results[:count], results[count:]
    backs, results = results[: 2 * count - 1], results[2 * count - 1 :]
    return outs, backs, results[:steps], results[steps:]


def sum_backs_kernel(*refs):
    own, rest, out_ref = refs[:2], refs[2:6], refs[6]
    total = own[0][...].astype(f32) + own[1][...].astype(f32)
    early = rest[0][...].astype(f32) + rest[2][...].astype(f32)
    late = rest[1][...].astype(f32) + rest[3][...].astype(f32)
    out_ref[...] = (total + jnp.where(pl.program_id(0) < GROUP // 2, early, late)).astype(bf16)


def sum_backs(own, came):
    _, full, width = own[0].shape
    spec = lambda index: pl.BlockSpec((1, full, width), lambda i: (index(i), 0, 0))
    first = spec(lambda i: jnp.minimum(i, GROUP // 2 - 1))
    second = spec(lambda i: jnp.maximum(i - GROUP // 2, 0))
    return pl.pallas_call(
        sum_backs_kernel,
        grid=(GROUP,),
        in_specs=[spec(lambda i: i)] * 2 + [first, second] * 2,
        out_specs=spec(lambda i: i),
        out_shape=jax.ShapeDtypeStruct((GROUP, full, width), bf16),
        compiler_params=params(32),
        name="sum_backs",
    )(*own, *came)


def trade(value, axis, bit):
    size = lax.axis_size(axis)
    return lax.ppermute(value, axis, [(i, i ^ bit) for i in range(size)])


def pick(value, index):
    return lax.dynamic_index_in_dim(value, index, axis=0, keepdims=False)


def after(value, *others):
    return lax.optimization_barrier((value, *others))[0]


def add_split_kernel(bit_ref, keep_other, came_other, keep_own, came_own, send_ref, own_ref):
    send_ref[...] = (keep_other[...].astype(f32) + came_other[...].astype(f32)).astype(bf16)
    own_ref[...] = (keep_own[...].astype(f32) + came_own[...].astype(f32)).astype(bf16)


def add_split(bit, keep, came):
    rows, width = came.shape
    tile = 128
    tiles = rows // 2 // tile
    other = pl.BlockSpec((tile, width), lambda i, bit: ((1 - bit[0]) * tiles + i, 0))
    own = pl.BlockSpec((tile, width), lambda i, bit: (bit[0] * tiles + i, 0))
    result = pl.BlockSpec((tile, width), lambda i, bit: (i, 0))
    return pl.pallas_call(
        add_split_kernel,
        grid_spec=pltpu.PrefetchScalarGridSpec(
            num_scalar_prefetch=1,
            grid=(tiles,),
            in_specs=[other, other, own, own],
            out_specs=[result, result],
        ),
        out_shape=[jax.ShapeDtypeStruct((rows // 2, width), bf16)] * 2,
        cost_estimate=hint(60),
        name="add_split",
    )(bit.reshape(1), keep, came, keep, came)


def add_pairs_kernel(a_ref, b_ref, c_ref, d_ref, *refs):
    out_ref = refs[-1]
    out_ref[0, 0] = (a_ref[...].astype(f32) + b_ref[...].astype(f32)).astype(bf16)
    out_ref[1, 0] = (c_ref[...].astype(f32) + d_ref[...].astype(f32)).astype(bf16)


def add_pairs(a, b, c, d, before):
    rows, width = a.shape
    tile = 128
    chunk = 0 if before is None else 1
    kept = () if before is None else (before,)
    return pl.pallas_call(
        add_pairs_kernel,
        grid=(rows // tile,),
        in_specs=[pl.BlockSpec((tile, width), lambda i: (i, 0))] * 4
        + [pl.BlockSpec(memory_space=pl.ANY)] * len(kept),
        out_specs=pl.BlockSpec((2, 1, tile, width), lambda i: (0, chunk, i, 0)),
        out_shape=jax.ShapeDtypeStruct((2, 2, rows, width), bf16),
        input_output_aliases={} if before is None else {4: 0},
        cost_estimate=hint(60),
        name="add_pairs",
    )(a, b, c, d, *kept)


def put_kernel(count, spots, *refs):
    pieces, refs = refs[:count], refs[-4:]
    gin_ref, gout_ref, buffer, sems = refs
    step, steps = pl.program_id(0), pl.num_programs(0)
    rows = buffer.shape[2]
    rest = FF - rows

    def each(at, index, slot, act):
        first = 3 * (index * steps + at)
        expert, half, quarter = spots[first], spots[first + 1], spots[first + 2]
        top = pl.multiple_of(half * FF, FF)

        @pl.when(quarter == 0)
        def _():
            act(
                pltpu.make_async_copy(
                    buffer.at[slot, index], gin_ref.at[expert, pl.ds(top, rows)], sems.at[slot, index, 0]
                )
            )

        @pl.when(quarter == 1)
        def _():
            act(
                pltpu.make_async_copy(
                    buffer.at[slot, index, pl.ds(0, rest)],
                    gin_ref.at[expert, pl.ds(pl.multiple_of(top + rows, rest), rest)],
                    sems.at[slot, index, 0],
                )
            )
            act(
                pltpu.make_async_copy(
                    buffer.at[slot, index, pl.ds(rest, rows - rest)],
                    gout_ref.at[expert, pl.ds(pl.multiple_of(half * (FF // 2), FF // 2), FF // 2)],
                    sems.at[slot, index, 1],
                )
            )

    slot = step % 2
    for index in range(count):

        @pl.when(step >= 2)
        def _():
            each(step - 2, index, slot, lambda copy: copy.wait())

        buffer[slot, index] = pieces[index][0, 0].astype(f32)
        each(step, index, slot, lambda copy: copy.start())

    @pl.when(step == steps - 1)
    def _():
        for index in range(count):
            each(steps - 2, index, 1 - slot, lambda copy: copy.wait())
            each(steps - 1, index, slot, lambda copy: copy.wait())


def put(spots, pieces, experts, before):
    paths, chunks, rows, width = pieces[0].shape
    kept = () if before is None else tuple(before)
    count, steps = len(pieces), paths * chunks
    anywhere = pl.BlockSpec(memory_space=pl.ANY)
    return pl.pallas_call(
        functools.partial(put_kernel, count),
        grid_spec=pltpu.PrefetchScalarGridSpec(
            num_scalar_prefetch=1,
            grid=(steps,),
            in_specs=[
                pl.BlockSpec((1, 1, rows, width), lambda i, c: (i // chunks, i % chunks, 0, 0))
            ]
            * count
            + [anywhere] * len(kept),
            out_specs=[anywhere] * 2,
            scratch_shapes=[
                pltpu.VMEM((2, count, rows, width), f32),
                pltpu.SemaphoreType.DMA((2, count, 2)),
            ],
        ),
        out_shape=[
            jax.ShapeDtypeStruct((experts, width, 2 * FF), f32),
            jax.ShapeDtypeStruct((experts, FF, width), f32),
        ],
        input_output_aliases={} if before is None else {1 + count: 0, 2 + count: 1},
        compiler_params=params(40),
        cost_estimate=hint(1),
        name="put",
    )(spots, *pieces, *kept)


def plane_parts(value, *between):
    half = value.shape[0] // 2
    along, across = trade(value, "row", 1), trade(value, "row", 2)
    there = trade(value, "col", 1)
    along, across = after((along, across), *between)
    far = jnp.concatenate(
        [trade(along[:half], "row", 2), trade(across[half:], "row", 1)], axis=0
    )
    return [value, along, across, far, there] + [
        trade(part, "col", 1) for part in (along, across, far)
    ]


def body(
    block_input,
    seq_lengths,
    routes,
    norm1_gain,
    w_qkv,
    w_heads,
    norm2_gain,
    router,
    w_expert_in,
    w_expert_out,
    out_grad,
):
    tok_rows, batches, width = block_input.shape
    dp_size = lax.axis_size("dp")
    plane = lax.axis_size("row") * lax.axis_size("col")
    packed = tok_rows * plane
    tokens = tok_rows * batches
    dp_at = lax.axis_index("dp").astype(jnp.int32)
    sds = jax.ShapeDtypeStruct

    x = jnp.transpose(block_input, (1, 0, 2)).reshape(tokens, width)
    og = jnp.transpose(out_grad, (1, 0, 2)).reshape(tokens, width)
    scale1 = lax.rsqrt(jnp.mean(x * x, axis=1, keepdims=True) + norm_eps)
    normed1 = (x * scale1 * norm1_gain).astype(bf16)
    flat_routes = jnp.transpose(routes, (1, 0, 2)).reshape(tokens, -1)
    used = jnp.any(
        flat_routes[None] == jnp.arange(EXPERTS, dtype=jnp.int32)[:, None, None], axis=2
    )
    before = (
        jnp.arange(tokens, dtype=jnp.int32)[:, None] < jnp.arange(tokens, dtype=jnp.int32)[None, :]
    )
    counted = jnp.dot(used.astype(bf16), before.astype(bf16), preferred_element_type=f32)
    rank = jnp.where(used, counted, -1.0).astype(bf16)
    rank_rows = jnp.transpose(rank.reshape(EXPERTS // 8, 8, tokens), (1, 0, 2)).reshape(8, -1)
    grads_in = lax.all_gather(
        jnp.concatenate([og.astype(bf16), rank_rows, jnp.zeros_like(rank_rows)], axis=0),
        "dp",
        axis=0,
        tiled=False,
    )

    segment, position = pack_tables(seq_lengths[0], packed)
    inverse = jnp.exp(
        -(2.0 * jnp.arange(HEAD_SIZE // 2, dtype=f32) / HEAD_SIZE) * math.log(rope_base)
    )
    angles = position.astype(f32)[:, :, None] * inverse[None, None, :]
    cosine, sine = jnp.cos(angles), jnp.sin(angles)
    cosine = jnp.concatenate([cosine] * 4, axis=2)
    sine = jnp.concatenate([-sine, sine, -sine, sine], axis=2)
    seg_rows, seg_cols = segment[:, :, None], segment[:, None, :]

    row = lax.axis_index("row").astype(jnp.int32)
    col = lax.axis_index("col").astype(jnp.int32)
    places = jnp.stack([(row ^ k) * 2 + (col ^ c) for c in range(2) for k in range(4)])
    w_group = lax.all_to_all(w_qkv, "col", split_axis=1, concat_axis=0, tiled=True)
    parts = plane_parts(
        normed1.reshape(batches, tok_rows, width), cosine, sine, seg_rows, seg_cols, w_group
    )

    per_m = lambda m, *_: (m, 0, 0)
    const = lambda m, *_: (0, 0)
    by_device = lambda m, *_: (0, m, 0, 0)
    table_specs = [
        pl.BlockSpec((1, packed, 128), per_m),
        pl.BlockSpec((1, packed, 128), per_m),
        pl.BlockSpec((1, packed, 1), per_m),
        pl.BlockSpec((1, 1, packed), per_m),
    ]
    x_all, qkv, head_out, lse = pl.pallas_call(
        attn_fwd_kernel,
        grid_spec=pltpu.PrefetchScalarGridSpec(
            num_scalar_prefetch=1,
            grid=(batches,),
            in_specs=[
                *[pl.BlockSpec((1, tok_rows, width), per_m)] * 8,
                pl.BlockSpec((width, 256), const),
                *table_specs,
            ],
            out_specs=[
                pl.BlockSpec((1, packed, width), per_m),
                pl.BlockSpec((1, packed, 256), per_m),
                pl.BlockSpec((plane, 1, tok_rows, 128), by_device),
                pl.BlockSpec((1, packed, 128), per_m),
            ],
            scratch_shapes=[pltpu.VMEM((packed, 256), f32)],
        ),
        out_shape=[
            sds((batches, packed, width), bf16),
            sds((batches, packed, 256), bf16),
            sds((plane, batches, tok_rows, 128), bf16),
            sds((batches, packed, 128), f32),
        ],
        compiler_params=params(48),
        cost_estimate=hint(13),
        name="attn_fwd",
    )(places, *parts, w_group, cosine, sine, seg_rows, seg_cols)

    heads = lax.all_to_all(
        head_out.reshape(plane, tokens, 128), PLANE, split_axis=0, concat_axis=0, tiled=True
    )
    gain1, gain2 = norm1_gain.reshape(1, width), norm2_gain.reshape(1, width)
    router_t = jnp.transpose(router)
    w_heads_parts = plane_parts(after(w_heads, parts[3]), head_out)

    def with_places(kernel, count, outs, mib, name):
        in_vmem = pl.BlockSpec(memory_space=pltpu.VMEM)
        return pl.pallas_call(
            kernel,
            in_specs=[pl.BlockSpec(memory_space=pltpu.SMEM)] + [in_vmem] * count,
            out_shape=outs,
            compiler_params=params(mib),
            name=name,
        )

    mixed, send, gates = with_places(
        token_fwd_kernel,
        13,
        [
            sds((tokens, width), f32),
            sds((tokens + TAIL, width), bf16),
            sds((EXPERTS, tokens), f32),
        ],
        32,
        "token_fwd",
    )(places, *w_heads_parts, heads, x, gain2, router_t, rank)

    rows_in = lax.all_gather(send, "dp", axis=0, tiled=False)
    w_group_parts = plane_parts(after(w_group, send))
    here = w_expert_in.shape[0]
    first, second = row % 2, (row // 2) % 2
    bits = jnp.stack([first, second])
    shared = here == 8
    chunks = []
    if shared:
        grads_there = trade(grads_in, "col", 1)
        rows_in = after(rows_in, w_group_parts, grads_there)
        rows_there = trade(rows_in, "col", 1)
        own_backs, came_backs, outs = [], [], []
        for index in range(2):
            begin = 4 * col + 2 * index
            out, back, away, kept = run_experts(
                dp_at * here + begin,
                begin,
                bits,
                ((rows_in, grads_in), (rows_there, grads_there)),
                w_expert_in,
                w_expert_out,
                2,
            )
            own_backs.append(back[0])
            came_backs += [trade(value, "col", 1) for value in back[1:]]
            outs += [out[0], trade(out[1], "col", 1)]
            chunks.append((away, kept))
            rows_there = after(rows_there, back[0])
            last = back[0]
    else:
        zero = jnp.zeros_like(dp_at)
        outs, (back,), away, kept = run_experts(
            dp_at * here,
            zero,
            jnp.zeros_like(bits),
            ((rows_in, grads_in),),
            w_expert_in,
            w_expert_out,
            1,
        )

    flips = (1, 2)
    halves = []

    def first_sum(away, kept, *order):
        kept = after(kept, *order)
        came = [trade(away[path], "row", flips[path]) for path in range(2)]
        return [add_split(bits[1 - path], kept[path], came[path]) for path in range(2)]

    def second_sum(halves, before, *order):
        came = [trade(halves[path][0], "row", flips[1 - path]) for path in range(2)]
        own = after((halves[0][1], halves[1][1]), *order)
        return add_pairs(own[0], came[0], own[1], came[1], before)

    if shared:
        halves.append(first_sum(*chunks[0], last))
        own_backs = after(own_backs, halves[0])
        back = sum_backs(own_backs, came_backs)
        halves.append(first_sum(*chunks[1], back))
        ready_a = second_sum(halves[0], None, halves[1])
    back = lax.psum_scatter(
        back.reshape(dp_size * (tokens + TAIL), width), "dp", scatter_dimension=0, tiled=True
    )
    if shared:
        back = after(back, ready_a)
    grad_mixed, grad_heads, sums = with_places(
        token_bwd_kernel,
        16,
        [
            sds((tokens, width), f32),
            sds((plane, tokens, 128), bf16),
            sds((plane, 128 + TAIL, width), bf16),
        ],
        40,
        "token_bwd",
    )(places, *w_heads_parts, back, mixed, og, gates, heads, gain2, router_t, send)
    sums = lax.psum_scatter(
        sums.reshape(plane * (128 + TAIL), width), PLANE, scatter_dimension=0, tiled=True
    )
    grad_heads = lax.all_to_all(grad_heads, PLANE, split_axis=0, concat_axis=0, tiled=True)

    if shared:
        ready_b = second_sum(halves[1], ready_a, grad_heads)
        grad_heads = after(grad_heads, ready_b)

    grad_joined, grad_w_qkv = pl.pallas_call(
        attn_bwd_kernel,
        grid=(batches,),
        in_specs=[
            pl.BlockSpec((1, packed, width), per_m),
            pl.BlockSpec((width, 256), const),
            *table_specs,
            pl.BlockSpec((1, packed, 256), per_m),
            pl.BlockSpec((1, packed, 128), per_m),
            pl.BlockSpec((plane, 1, tok_rows, 128), by_device),
        ],
        out_specs=[
            pl.BlockSpec((plane, 1, tok_rows, 256), by_device),
            pl.BlockSpec((2, width // 2 + TAIL, 256), lambda m: (0, 0, 0)),
        ],
        out_shape=[
            sds((plane, batches, tok_rows, 256), bf16),
            sds((2, width // 2 + TAIL, 256), bf16),
        ],
        scratch_shapes=[
            pltpu.VMEM((width, 256), f32),
            pltpu.VMEM((packed, 128), f32),
            pltpu.VMEM((packed, 128), f32),
        ],
        compiler_params=params(48),
        cost_estimate=hint(18),
        name="attn_bwd",
    )(
        x_all, w_group, cosine, sine, seg_rows, seg_cols, qkv, lse,
        grad_heads.reshape(plane, batches, tok_rows, 128),
    )

    if shared:
        along, across = trade(ready_b, "row", 1), trade(ready_b, "row", 2)
    grad_joined = lax.all_to_all(
        grad_joined.reshape(plane, tokens, 256), PLANE, split_axis=0, concat_axis=0, tiled=True
    )
    grad_w_qkv = lax.all_to_all(grad_w_qkv, "col", split_axis=0, concat_axis=0, tiled=True)
    produced = sum(value.astype(f32) for value in outs).astype(bf16)
    sums, produced = lax.optimization_barrier((sums, produced))
    sums, grad_w_qkv = lax.psum((sums, grad_w_qkv), "dp")
    produced = lax.psum_scatter(
        produced.reshape(dp_size * tokens, width), "dp", scatter_dimension=0, tiled=True
    )
    block_output = mixed + produced.astype(f32)
    if shared:
        along, across = after((along, across), grad_joined)
        fars = (trade(across[:1], "row", 1), trade(along[1:], "row", 2))
    input_grad = with_places(token_end_kernel, 12, sds((tokens, width), f32), 32, "token_end")(
        places, *w_group_parts, grad_joined, x, gain1, grad_mixed
    )

    if shared:
        fronts = (ready_b, along, across)
        fronts_there = tuple(trade(value, "col", 1) for value in fronts)

        def spots(owner, path, chunk, k):
            pair = (first ^ (k & 1), second ^ (k >> 1))
            return [4 * owner + 2 * chunk + path, pair[path], pair[1 - path]]

        def front_spots(owner):
            return jnp.stack(
                [v for k in range(3) for p in range(2) for c in range(2) for v in spots(owner, p, c, k)]
            )

        def far_spots(owner):
            return jnp.stack([v for p in range(2) for c in range(2) for v in spots(owner, p, c, 3)])

        first_put = put(front_spots(col), fronts, here, None)
        grad_experts = put(front_spots(1 - col), fronts_there, here, first_put)
        sums, grad_w_qkv = after((sums, grad_w_qkv), grad_experts)

    sums = sums.astype(f32)
    heads_grad = sums[:128]
    half = width // 2
    qkv_sums = grad_w_qkv.astype(f32)
    grad_w_qkv = jnp.concatenate([qkv_sums[0, :half], qkv_sums[1, :half]], axis=1)
    scaled = qkv_sums[:, half : half + 4] + qkv_sums[:, half + 4 : half + 8]
    scaled = jnp.sum(scaled, axis=0).reshape(1, width)
    rest = plane_parts(
        jnp.concatenate([scaled, sums[128:], jnp.zeros((15, width), f32)], axis=0)
    )
    per = EXPERTS // plane
    norm1_grad = sum(part[0] for part in rest[:4]) / norm1_gain
    norm2_grad = sum(part[1 + per] for part in rest)
    router_grad = sum(
        jnp.where(
            places[index] == jnp.arange(plane, dtype=jnp.int32)[:, None, None],
            part[None, 1 : 1 + per],
            0.0,
        )
        for index, part in enumerate(rest)
    )
    router_grad = jnp.transpose(router_grad.reshape(EXPERTS, width))

    if shared:
        fars = after(fars, grad_experts)
        fars_there = tuple(trade(value, "col", 1) for value in fars)
        grad_experts = put(far_spots(col), fars, here, grad_experts)
        grad_experts = after(grad_experts, block_output, heads_grad, grad_w_qkv, input_grad)
        grad_experts = put(far_spots(1 - col), fars_there, here, grad_experts)
        grad_w_in, grad_w_out = grad_experts
    else:
        total = lax.psum(jnp.stack([kept[0], away[0]]), PLANE).astype(f32)
        total = total.reshape(here, 2, (width + FF) // 2, width)
        grad_w_in = total[:, :, : width // 2].reshape(here, width, 2 * FF)
        grad_w_out = total[:, :, width // 2 :].reshape(here, FF, width)

    def placed(value):
        return jnp.transpose(value.reshape(batches, tok_rows, width), (1, 0, 2))

    return (
        placed(block_output),
        placed(input_grad),
        norm1_grad,
        grad_w_qkv,
        heads_grad,
        norm2_grad,
        router_grad,
        grad_w_in,
        grad_w_out,
    )


def solution(mesh):
    return jax.shard_map(
        body,
        mesh=mesh,
        in_specs=(
            P(("dp", "row", "col"), None, None),
            P("dp", None, None),
            P(("dp", "row", "col"), None, None),
            P(),
            P("col", "row"),
            P(("row", "col"), None),
            P(),
            P(),
            P("dp", None, None),
            P("dp", None, None),
            P(("dp", "row", "col"), None, None),
        ),
        out_specs=(
            P(("dp", "row", "col"), None, None),
            P(("dp", "row", "col"), None, None),
            P(),
            P("col", "row"),
            P(("row", "col"), None),
            P(),
            P(),
            P("dp", None, None),
            P("dp", None, None),
        ),
        check_vma=False,
    )
```
